128 devices in a mesh: row: 8 (over y, z_lo), col: 16 (over x, z_hi, core).
Axes of the slice: x: 4, y: 4, z: 4 (z_hi: 2, z_lo: 2; z = z_hi * 2 + z_lo), core: 2. Of those that a mesh axis runs over, the one named last changes fastest.
Arguments:
- tokens: bfloat16 [2048, 8192], P('col', 'row'), may hold values from -6 to 6
- w1_blocks: bfloat16 [8, 16, 8, 256, 256], P('row', 'col'), may hold values from -0.1875 to 0.1875
- w2_blocks: bfloat16 [16, 8, 8, 256, 256], P('col', 'row'), may hold values from -0.09375 to 0.09375
- block_places: int32 [8, 16, 8], P('row', 'col'), may hold values from 0 to 31, as said below
- counts: int32 [8, 16], P('row', 'col'), may hold values from 1 to 8
- cotangent: bfloat16 [2048, 8192], P('col', 'row'), may hold values from -6 to 6
Outputs:
- output: bfloat16 [2048, 8192], P('col', 'row')
- input_grad: bfloat16 [2048, 8192], P('col', 'row')
- first_grad: bfloat16 [8, 16, 8, 256, 256], P('row', 'col')
- second_grad: bfloat16 [16, 8, 8, 256, 256], P('col', 'row')
The draws below stay inside these ranges and needn't reach their ends.
Inputs may be any that keep to these rules, and one draw needn't show every extreme that they name: `block_places`: within each tile the 8 positions are distinct; position p stands for the tile's model-width block p // 8 and hidden block p % 8; only the first counts of them are live.
All inputs are finite; a program needn't handle non-finite values.
Results may differ from the reference program's by a relative error of at most 0.025.
Values may be sent and summed in bfloat16 or wider, within the bound.
A program may use at most 128 MiB of HBM per device.

```python
import math
import jax
import jax.numpy as jnp
from jax import lax

D = 8192
F = 32768
BLK = 256
TOKENS = 2048
DBLK = 4
FBLK = 8
KMAX = 8
N_ROW = 8
N_COL = 16


def draw_counts(key, part):
    key = jax.random.fold_in(key, 11)
    first_key, second_key = jax.random.split(key)
    base_counts = jax.random.randint(first_key, (N_ROW * N_COL,), 1, KMAX + 1)
    chosen = jax.random.randint(second_key, (), 0, N_ROW * N_COL)
    flat_counts = jnp.where(jnp.arange(N_ROW * N_COL) == chosen, KMAX, base_counts)
    return flat_counts.reshape(N_ROW, N_COL).astype(jnp.int32)


def draw_block_places(key, part):
    key = jax.random.fold_in(key, 23)
    tile_keys = jax.random.split(key, N_ROW * N_COL)
    shuffled = jax.vmap(lambda tile_key: jax.random.permutation(tile_key, DBLK * FBLK))(tile_keys)
    return shuffled[:, :KMAX].reshape(N_ROW, N_COL, KMAX).astype(jnp.int32)


def levels(own_key, extent, pieces, smallest, top_value):
    gain, own = 1.0, jax.random.fold_in(own_key, 6)
    for dim, parts in pieces:
        steps = jnp.exp(jax.random.uniform(jax.random.fold_in(own, dim), (parts,), jnp.float32, smallest / len(pieces), top_value / len(pieces)))
        gain = gain * jnp.repeat(steps, extent[dim] // parts).reshape([-1 if axis == dim else 1 for axis in range(len(extent))])
    return gain


def centred(stream_key, extent, scale, bound, cuts=(), kind=jnp.bfloat16):
    array = scale * jax.random.normal(stream_key, extent, jnp.float32)
    if cuts:
        array = array * levels(stream_key, extent, cuts, -0.22, 0.18)
    return jnp.clip(array, -bound, bound).astype(kind)


def setup_inputs(seed: int = 0) -> dict:
    splits = jax.random.split(jax.random.key(seed), 7)
    return {
        "tokens": centred(splits[0], (TOKENS, D), 1.0, 6.0, ((0, 16), (1, 8))),
        "w1_blocks": centred(splits[1], (N_ROW, N_COL, KMAX, BLK, BLK), (D // 8) ** -0.5, 0.1875, ((0, 8), (1, 16))),
        "w2_blocks": centred(splits[2], (N_COL, N_ROW, KMAX, BLK, BLK), (F // 8) ** -0.5, 0.09375, ((0, 16), (1, 8))),
        "block_places": draw_block_places(jax.random.fold_in(splits[6], 71), 0),
        "counts": draw_counts(jax.random.fold_in(splits[6], 71), 0),
        "cotangent": centred(splits[5], (TOKENS, D), 1.0, 6.0, ((0, 16), (1, 8))),
    }


gelu_scale = math.sqrt(2.0 / math.pi)
gelu_cubic = 0.044715

def gelu_pair(hidden):
    inner = gelu_scale * (hidden + gelu_cubic * hidden * hidden * hidden)
    tanh_value = jnp.tanh(inner)
    value = 0.5 * hidden * (1.0 + tanh_value)
    slope = 0.5 * (1.0 + tanh_value) + 0.5 * hidden * (1.0 - tanh_value * tanh_value) * gelu_scale * (1.0 + 3.0 * gelu_cubic * hidden * hidden)
    return (value, slope)

def block_sum(source, weights, source_block, target_block, live, width, flipped):

    def advance(total, item):
        weight, from_block, to_block, active = item
        columns = lax.dynamic_slice_in_dim(source, from_block * BLK, BLK, 1)
        if flipped:
            product = lax.dot_general(columns, weight, (((1,), (1,)), ((), ())), preferred_element_type=jnp.float32)
        else:
            product = jnp.dot(columns, weight, preferred_element_type=jnp.float32)
        current = lax.dynamic_slice_in_dim(total, to_block * BLK, BLK, 1)
        return (lax.dynamic_update_slice_in_dim(total, current + product * active, to_block * BLK, 1), None)
    start = jnp.zeros((source.shape[0], width), jnp.float32)
    total, unused = lax.scan(advance, start, (weights, source_block, target_block, live))
    return total

def rounded(values):
    return lax.optimization_barrier(values.astype(jnp.bfloat16)).astype(jnp.float32)

def slot_grads(left, right, left_block, right_block, live):

    def single(item):
        from_block, to_block, active = item
        left_cols = lax.dynamic_slice_in_dim(left, from_block * BLK, BLK, 1)
        right_cols = lax.dynamic_slice_in_dim(right, to_block * BLK, BLK, 1)
        product = lax.dot_general(left_cols, right_cols, (((0,), (0,)), ((), ())), preferred_element_type=jnp.float32)
        return (product * active).astype(jnp.bfloat16)
    return lax.map(single, (left_block, right_block, live))

def reference(tokens, w1_blocks, w2_blocks, block_places, counts, cotangent):
    slot_range = jnp.arange(KMAX, dtype=jnp.int32)
    live_all = (slot_range[None, None, :] < counts[:, :, None]).astype(jnp.float32)
    row_ids = jnp.arange(N_ROW, dtype=jnp.int32)[:, None, None]
    col_ids = jnp.arange(N_COL, dtype=jnp.int32)[None, :, None]
    model_global = (row_ids * DBLK + block_places // FBLK).astype(jnp.int32)
    hidden_global = (col_ids * FBLK + block_places % FBLK).astype(jnp.int32)
    w2_by_tile = jnp.transpose(w2_blocks, (1, 0, 2, 3, 4))
    hidden_sum = jnp.zeros((TOKENS, F), jnp.float32)
    for row_index in range(N_ROW):
        partial_sum = block_sum(tokens, w1_blocks[row_index].reshape(-1, BLK, BLK), model_global[row_index].reshape(-1), hidden_global[row_index].reshape(-1), live_all[row_index].reshape(-1), F, False)
        hidden_sum = hidden_sum + rounded(partial_sum)
    gelu_value, gelu_slope = gelu_pair(hidden_sum)
    activated = gelu_value.astype(jnp.bfloat16)
    output_sum = jnp.zeros((TOKENS, D), jnp.float32)
    for col_index in range(N_COL):
        partial_sum = block_sum(activated, w2_by_tile[:, col_index].reshape(-1, BLK, BLK), hidden_global[:, col_index].reshape(-1), model_global[:, col_index].reshape(-1), live_all[:, col_index].reshape(-1), D, False)
        output_sum = output_sum + rounded(partial_sum)
    output = output_sum.astype(jnp.bfloat16)
    grad_sum = jnp.zeros((TOKENS, F), jnp.float32)
    for row_index in range(N_ROW):
        partial_sum = block_sum(cotangent, w2_by_tile[row_index].reshape(-1, BLK, BLK), model_global[row_index].reshape(-1), hidden_global[row_index].reshape(-1), live_all[row_index].reshape(-1), F, True)
        grad_sum = grad_sum + rounded(partial_sum)
    hidden_grad = (grad_sum * gelu_slope).astype(jnp.bfloat16)
    input_sum = jnp.zeros((TOKENS, D), jnp.float32)
    for col_index in range(N_COL):
        partial_sum = block_sum(hidden_grad, w1_blocks[:, col_index].reshape(-1, BLK, BLK), hidden_global[:, col_index].reshape(-1), model_global[:, col_index].reshape(-1), live_all[:, col_index].reshape(-1), D, True)
        input_sum = input_sum + rounded(partial_sum)
    input_grad = input_sum.astype(jnp.bfloat16)
    first_grad = slot_grads(tokens, hidden_grad, model_global.reshape(-1), hidden_global.reshape(-1), live_all.reshape(-1))
    first_grad = first_grad.reshape(N_ROW, N_COL, KMAX, BLK, BLK)
    second_grad = slot_grads(activated, cotangent, hidden_global.reshape(-1), model_global.reshape(-1), live_all.reshape(-1))
    second_grad = jnp.transpose(second_grad.reshape(N_ROW, N_COL, KMAX, BLK, BLK), (1, 0, 2, 3, 4))
    return (output, input_grad, first_grad, second_grad)
```

```python
import functools
import math

import jax
import jax.numpy as jnp
from jax import lax
from jax.experimental import pallas as pl
from jax.experimental.pallas import tpu as pltpu
from jax.sharding import PartitionSpec as P

BLK = 256
SLOTS = 8
HIDDEN_BLOCKS = 8
QUARTER = 32
WIDTH = 1024
ROWS = 512
bf16 = jnp.bfloat16
f32 = jnp.float32

gelu_scale = math.sqrt(2.0 / math.pi)
gelu_cubic = 0.044715
MIB = 1 << 20


def gelu_pair(hidden):
    inner = gelu_scale * (hidden + gelu_cubic * hidden * hidden * hidden)
    tanh_value = jnp.tanh(inner)
    value = 0.5 * hidden * (1.0 + tanh_value)
    slope = 0.5 * (1.0 + tanh_value) + 0.5 * hidden * (
        1.0 - tanh_value * tanh_value
    ) * gelu_scale * (1.0 + 3.0 * gelu_cubic * hidden * hidden)
    return (value, slope)


def y_index():
    return lax.div(lax.axis_index("row"), 2)


def peer(dx=0, dy=0, zl=0, zh=0, core=0):
    k, j = lax.axis_index("row"), lax.axis_index("col")
    row = lax.rem(lax.div(k, 2) + dy, 4) * 2 + lax.rem(lax.rem(k, 2) + zl, 2)
    col = (
        lax.rem(lax.div(j, 4) + dx, 4) * 4
        + lax.rem(lax.rem(lax.div(j, 2), 2) + zh, 2) * 2
        + lax.rem(lax.rem(j, 2) + core, 2)
    )
    return (row, col)


Y_PEERS = [dict(dy=1), dict(dy=2), dict(dy=3)]
X_PEERS = [dict(dx=1), dict(dx=3)]
CORE_PEER, ZH_PEER, ZL_PEER = dict(core=1), dict(zh=1), dict(zl=1)


def greet(peers):
    barrier = pltpu.get_barrier_semaphore()
    for one in peers:
        pl.semaphore_signal(barrier, inc=1, device_id=peer(**one), device_id_type=pl.DeviceIdType.MESH)
    pl.semaphore_wait(barrier, len(peers))


class Copies:
    def __init__(self, send, recv):
        self.send, self.recv, self.made = send, recv, []

    def start(self, src, dst, **to):
        n = len(self.made)
        copy = pltpu.make_async_remote_copy(
            src_ref=src, dst_ref=dst, send_sem=self.send.at[n], recv_sem=self.recv.at[n],
            device_id=peer(**to), device_id_type=pl.DeviceIdType.MESH,
        )
        copy.start()
        self.made.append(copy)
        return copy

    def finish(self):
        for copy in self.made:
            copy.wait_send()


def ring_gather_start(copies, own, dest, axis):
    up, down = {axis: 1}, {axis: 3}
    half = own.shape[0] // 2
    lo, hi = pl.ds(0, half), pl.ds(half, half)
    up_lo = copies.start(own.at[lo], dest.at[3, lo], **up)
    down_hi = copies.start(own.at[hi], dest.at[1, hi], **down)
    up_hi = copies.start(own.at[hi], dest.at[3, hi], **up)
    down_lo = copies.start(own.at[lo], dest.at[1, lo], **down)
    return (up_lo, down_hi, up_hi, down_lo)


def ring_gather_forward(copies, begun, dest, axis):
    up, down = {axis: 1}, {axis: 3}
    half = dest.shape[1] // 2
    lo, hi = pl.ds(0, half), pl.ds(half, half)
    begun[0].wait_recv()
    on_up = copies.start(dest.at[3, lo], dest.at[2, lo], **up)
    begun[1].wait_recv()
    on_down = copies.start(dest.at[1, hi], dest.at[2, hi], **down)
    return (begun[2], begun[3], on_up, on_down)


def rows_of(core, x, zh):
    return ((core * 4 + x) * 2 + zh) * QUARTER


def gather_kernel(tok, cot, w1, tab, tok_all, cot_all, w1_all, tab_all, send, recv, local):
    greet(Y_PEERS + X_PEERS + [CORE_PEER, ZH_PEER])
    copies = Copies(send, recv)
    y = y_index()
    pairs = ((tok, tok_all), (cot, cot_all))
    half = pl.ds(0, QUARTER)
    locals_ = []
    for n, (src, dst) in enumerate(pairs):
        rows = pl.ds(pl.multiple_of(y * QUARTER, QUARTER), QUARTER)
        locals_.append(pltpu.make_async_copy(src.at[rows], dst.at[0, half], local.at[n]))
    locals_.append(pltpu.make_async_copy(w1, w1_all.at[0], local.at[2]))
    locals_.append(pltpu.make_async_copy(tab, tab_all.at[0], local.at[3]))
    for copy in locals_:
        copy.start()
    spread = []
    for src, dst in pairs:
        here = []
        for r in (1, 3, 2):
            rows = pl.ds(pl.multiple_of(lax.rem(y + r, 4) * QUARTER, QUARTER), QUARTER)
            here.append(copies.start(src.at[rows], dst.at[4 - r, half], dy=r))
        spread.append(here)
    tabs = [copies.start(tab, tab_all.at[4 - r], dy=r) for r in (1, 2, 3)]
    w_begun = ring_gather_start(copies, w1, w1_all, "dy")

    def part(core, x, zh, count=1):
        return (slice(None), pl.ds(rows_of(core, x, zh), count * QUARTER))

    across, first = [], []
    for n, (src, dst) in enumerate(pairs):
        locals_[n].wait()
        for copy in spread[n]:
            copy.wait_recv()
        own = dst.at[part(0, 0, 0)]
        across.append(copies.start(own, dst.at[part(0, 0, 1)], zh=1))
        first.append((
            copies.start(own, dst.at[part(0, 3, 0)], dx=1),
            copies.start(own, dst.at[part(0, 1, 0)], dx=3),
        ))
    second, over = [], []
    for n, (src, dst) in enumerate(pairs):
        across[n].wait_recv()
        own = dst.at[part(0, 0, 1)]
        second.append((
            copies.start(own, dst.at[part(0, 3, 1)], dx=1),
            copies.start(own, dst.at[part(0, 1, 1)], dx=3),
        ))
        over.append(copies.start(dst.at[part(0, 0, 0, 2)], dst.at[part(1, 0, 0, 2)], core=1))
    w_rest = ring_gather_forward(copies, w_begun, w1_all, "dy")
    onward = []
    for n, (src, dst) in enumerate(pairs):
        first[n][0].wait_recv()
        on_up = copies.start(dst.at[part(0, 3, 0)], dst.at[part(0, 2, 0)], dx=1)
        second[n][1].wait_recv()
        on_down = copies.start(dst.at[part(0, 1, 1)], dst.at[part(0, 2, 1)], dx=3)
        onward.append((on_up, on_down))
    for n, (src, dst) in enumerate(pairs):
        second[n][0].wait_recv()
        over.append(copies.start(dst.at[part(0, 3, 0, 2)], dst.at[part(1, 3, 0, 2)], core=1))
        first[n][1].wait_recv()
        over.append(copies.start(dst.at[part(0, 1, 0, 2)], dst.at[part(1, 1, 0, 2)], core=1))
    for n, (src, dst) in enumerate(pairs):
        for copy in onward[n]:
            copy.wait_recv()
        over.append(copies.start(dst.at[part(0, 2, 0, 2)], dst.at[part(1, 2, 0, 2)], core=1))
    for copy in tabs + over + list(w_rest):
        copy.wait_recv()
    locals_[2].wait()
    locals_[3].wait()
    copies.finish()


def exchange_start(copies, own, other):
    step = own.shape[0] // 4
    return [
        copies.start(own.at[pl.ds(n * step, step)], other.at[pl.ds(n * step, step)], zl=1)
        for n in range(4)
    ]


def second_kernel(w2, part, w2_all, other, send, recv, local):
    greet([dict(dy=1), dict(dy=3), ZL_PEER])
    copies = Copies(send, recv)
    mine = pltpu.make_async_copy(w2, w2_all.at[0], local.at[0])
    mine.start()
    begun = ring_gather_start(copies, w2, w2_all, "dy")
    swap = exchange_start(copies, part, other)
    rest = ring_gather_forward(copies, begun, w2_all, "dy")
    for copy in list(rest) + swap:
        copy.wait_recv()
    mine.wait()
    copies.finish()


def add_into(dst, *terms):
    def step(n, carry):
        total = terms[0][n].astype(f32)
        for term in terms[1:]:
            total = total + term[n].astype(f32)
        dst[n] = total.astype(dst.dtype)
        return carry

    lax.fori_loop(0, dst.shape[0], step, 0)


class RingReduce:
    def __init__(self, copies, part, far, near, axis):
        self.copies, self.part, self.far, self.near = copies, part, far, near
        self.up, self.down = {axis: 1}, {axis: 3}

    def start_far(self):
        self.far_up = self.copies.start(self.part(2, 0), self.far.at[0], **self.up)
        self.far_down = self.copies.start(self.part(2, 1), self.far.at[1], **self.down)

    def start_near(self):
        self.near_up = self.copies.start(self.part(1, 1), self.near.at[0, 1], **self.up)
        self.near_down = self.copies.start(self.part(3, 0), self.near.at[1, 0], **self.down)

    def onward(self):
        self.far_up.wait_recv()
        add_into(self.far.at[0], self.far.at[0], self.part(1, 0))
        self.last_up = self.copies.start(self.far.at[0], self.near.at[0, 0], **self.up)
        self.far_down.wait_recv()
        add_into(self.far.at[1], self.far.at[1], self.part(3, 1))
        self.last_down = self.copies.start(self.far.at[1], self.near.at[1, 1], **self.down)

    def finish(self, dst):
        for copy in (self.near_up, self.near_down, self.last_up, self.last_down):
            copy.wait_recv()
        for h in range(2):
            add_into(dst(h), self.part(0, h), self.near.at[0, h], self.near.at[1, h])


def weight_part(partial):
    return lambda r, h: partial.at[r, pl.ds(h * 4, 4)]


class OutputReduce:
    def __init__(self, copies, partial, arrived, far, near):
        self.copies, self.partial, self.arrived = copies, partial, arrived
        self.ring = RingReduce(
            copies, lambda r, h: arrived.at[:, pl.ds(r * 64 + h * 32, 32)], far, near, "dx")

    def start(self):
        self.over = {}
        for r in (2, 1, 3, 0):
            self.over[r] = self.copies.start(
                self.partial.at[:, pl.ds(256 + 64 * r, 64)], self.arrived.at[:, pl.ds(64 * r, 64)], core=1)

    def join(self, r):
        self.over[r].wait_recv()
        rows = pl.ds(64 * r, 64)
        add_into(self.arrived.at[:, rows], self.arrived.at[:, rows], self.partial.at[:, rows])

    def begin_ring(self):
        self.join(2)
        self.ring.start_far()
        self.join(1)
        self.join(3)
        self.ring.start_near()
        self.join(0)


def reduce_kernel(grad_part, second_part, out_part, grad_other, second_grad, out_mid,
                  far_w, near_w, arrived, far_x, near_x, send, recv):
    greet([dict(dy=1), dict(dy=3), ZL_PEER, CORE_PEER] + X_PEERS)
    copies = Copies(send, recv)
    weights = RingReduce(copies, weight_part(second_part), far_w, near_w, "dy")
    weights.start_far()
    swap = exchange_start(copies, grad_part, grad_other)
    out = OutputReduce(copies, out_part, arrived, far_x, near_x)
    out.start()
    weights.start_near()
    out.begin_ring()
    weights.onward()
    out.ring.onward()
    out.ring.finish(lambda h: out_mid.at[:, pl.ds(32 * h, 32)])
    weights.finish(lambda h: second_grad.at[pl.ds(4 * h, 4)])
    for copy in swap:
        copy.wait_recv()
    copies.finish()


class Home:
    def __init__(self, copies, mid, arrived, output, local):
        self.copies, self.mid, self.arrived, self.output, self.local = copies, mid, arrived, output, local

    def start(self):
        self.over = self.copies.start(self.mid.at[:, pl.ds(32, 32)], self.arrived, zh=1)

    def send(self):
        self.over.wait_recv()
        add_into(self.arrived, self.arrived, self.mid.at[:, pl.ds(0, 32)])
        rows = pl.ds(pl.multiple_of(y_index() * QUARTER, QUARTER), QUARTER)
        self.mine = pltpu.make_async_copy(self.arrived.at[0], self.output.at[rows], self.local)
        self.mine.start()
        self.sent = [self.copies.start(self.arrived.at[r], self.output.at[rows], dy=r) for r in (2, 1, 3)]

    def finish(self):
        self.mine.wait()
        for copy in self.sent:
            copy.wait_recv()


def last_kernel(first_part, in_part, out_mid, first_grad, output, input_grad,
                far_w, near_w, arrived, far_x, near_x, in_mid, home_out, home_in, send, recv, local):
    greet(Y_PEERS + X_PEERS + [CORE_PEER, ZH_PEER])
    copies = Copies(send, recv)
    weights = RingReduce(copies, weight_part(first_part), far_w, near_w, "dy")
    weights.start_far()
    into = OutputReduce(copies, in_part, arrived, far_x, near_x)
    into.start()
    out_home = Home(copies, out_mid, home_out, output, local.at[0])
    out_home.start()
    weights.start_near()
    into.begin_ring()
    out_home.send()
    weights.onward()
    into.ring.onward()
    into.ring.finish(lambda h: in_mid.at[:, pl.ds(32 * h, 32)])
    in_home = Home(copies, in_mid, home_in, input_grad, local.at[1])
    in_home.start()
    in_home.send()
    weights.finish(lambda h: first_grad.at[pl.ds(4 * h, 4)])
    out_home.finish()
    in_home.finish()
    copies.finish()


def columns(d):
    return pl.ds(pl.multiple_of(d * BLK, BLK), BLK)


def dot(a, b, da, db):
    return lax.dot_general(a, b, (((da,), (db,)), ((), ())), preferred_element_type=f32)


def hidden_kernel(tab, tok, w1, out, total):
    t = pl.program_id(0)

    @pl.when(t == 0)
    def _():
        total[...] = jnp.zeros_like(total)

    def step(s, carry):
        place = tab[t, 0, s]
        d, h = lax.div(place, HIDDEN_BLOCKS), lax.rem(place, HIDDEN_BLOCKS)
        total[h] += dot(tok[0, :, columns(d)], w1[0, s], 1, 0)
        return carry

    lax.fori_loop(0, tab[t, 0, SLOTS], step, 0)

    @pl.when(t == 3)
    def _():
        out[...] = total[...].astype(bf16)


CHUNK = 64


def forward_kernel(tab, mine, other, cot, w2, grad_part, out_part, second_part, slope, act, grad, out):
    t = pl.program_id(0)

    @pl.when(t == 0)
    def _():
        grad[...] = jnp.zeros_like(grad)

        def activate(n, carry):
            h, rows = lax.div(n, ROWS // CHUNK), pl.ds(pl.multiple_of(lax.rem(n, ROWS // CHUNK) * CHUNK, CHUNK), CHUNK)
            value, derivative = gelu_pair(mine[h, rows].astype(f32) + other[h, rows].astype(f32))
            act[h, rows] = value.astype(bf16)
            slope[h, rows] = derivative
            return carry

        lax.fori_loop(0, HIDDEN_BLOCKS * (ROWS // CHUNK), activate, 0)

    out[...] = jnp.zeros_like(out)

    def step(s, carry):
        place = tab[t, 0, s]
        d, h = lax.div(place, HIDDEN_BLOCKS), lax.rem(place, HIDDEN_BLOCKS)
        live = act[h]
        back = cot[0, :, columns(d)]
        weight = w2[0, s]
        grad[h] += dot(back, weight, 1, 1)
        out[:, columns(d)] += dot(live, weight, 1, 0)
        second_part[0, s] = dot(live, back, 0, 0).astype(bf16)
        return carry

    def dead(s, carry):
        second_part[0, s] = jnp.zeros((BLK, BLK), bf16)
        return carry

    count = tab[t, 0, SLOTS]
    lax.fori_loop(0, count, step, 0)
    lax.fori_loop(count, SLOTS, dead, 0)
    out_part[0] = out[...].astype(bf16)

    @pl.when(t == 3)
    def _():
        grad_part[...] = grad[...].astype(bf16)


def backward_kernel(tab, mine, other, slope, tok, w1, in_part, first_part, grad, out):
    t = pl.program_id(0)

    @pl.when(t == 0)
    def _():

        def combine(n, carry):
            h, rows = lax.div(n, ROWS // CHUNK), pl.ds(pl.multiple_of(lax.rem(n, ROWS // CHUNK) * CHUNK, CHUNK), CHUNK)
            total = mine[h, rows].astype(f32) + other[h, rows].astype(f32)
            grad[h, rows] = (total * slope[h, rows]).astype(bf16)
            return carry

        lax.fori_loop(0, HIDDEN_BLOCKS * (ROWS // CHUNK), combine, 0)

    out[...] = jnp.zeros_like(out)

    def step(s, carry):
        place = tab[t, 0, s]
        d, h = lax.div(place, HIDDEN_BLOCKS), lax.rem(place, HIDDEN_BLOCKS)
        back = grad[h]
        out[:, columns(d)] += dot(back, w1[0, s], 1, 1)
        first_part[0, s] = dot(tok[0, :, columns(d)], back, 0, 0).astype(bf16)
        return carry

    def dead(s, carry):
        first_part[0, s] = jnp.zeros((BLK, BLK), bf16)
        return carry

    count = tab[t, 0, SLOTS]
    lax.fori_loop(0, count, step, 0)
    lax.fori_loop(count, SLOTS, dead, 0)
    in_part[0] = out[...].astype(bf16)


ANY = pl.BlockSpec(memory_space=pl.ANY)
VMEM = pl.BlockSpec(memory_space=pltpu.VMEM)
SMEM = pl.BlockSpec(memory_space=pltpu.SMEM)
HIDDEN = (HIDDEN_BLOCKS, ROWS, BLK)
TILE = (SLOTS, BLK, BLK)
MODEL = (4, ROWS, WIDTH)
DMA = pltpu.SemaphoreType.DMA


def shape(dims, kind=bf16):
    return jax.ShapeDtypeStruct(dims, kind)


def whole(dims):
    return pl.BlockSpec(dims, lambda t: (0,) * len(dims))


def one_of(dims):
    return pl.BlockSpec((1,) + dims, lambda t: (t,) + (0,) * len(dims))


def talk(number, mib=16):
    return pltpu.CompilerParams(collective_id=number, has_side_effects=True, vmem_limit_bytes=mib * MIB)


def compute(kernel, in_specs, out_specs, out_shape, scratch, *args):
    return pl.pallas_call(
        kernel, grid=(4,), in_specs=in_specs, out_specs=out_specs, out_shape=out_shape, scratch_shapes=scratch,
        compiler_params=pltpu.CompilerParams(vmem_limit_bytes=56 * MIB, dimension_semantics=("arbitrary",)),
    )(*args)


def reduce_scratch():
    return [
        pltpu.VMEM((2, 4, BLK, BLK), bf16),
        pltpu.VMEM((2, 2, 4, BLK, BLK), bf16),
        pltpu.VMEM((4, 256, WIDTH), bf16),
        pltpu.VMEM((2, 4, 32, WIDTH), bf16),
        pltpu.VMEM((2, 2, 4, 32, WIDTH), bf16),
    ]


def per_device(tokens, w1_blocks, w2_blocks, block_places, counts, cotangent):
    w1, w2 = w1_blocks[0, 0], w2_blocks[0, 0]
    row = jnp.concatenate([block_places[0, 0], counts[0], jnp.zeros((128 - SLOTS - 1,), jnp.int32)])
    table = jnp.broadcast_to(row[None], (8, 128))

    tok_all, cot_all, w1_all, tab_all = pl.pallas_call(
        gather_kernel,
        out_shape=(shape(MODEL), shape(MODEL), shape((4,) + TILE), shape((4, 8, 128), jnp.int32)),
        in_specs=[ANY] * 4, out_specs=[ANY] * 4,
        scratch_shapes=[DMA((40,)), DMA((40,)), DMA((4,))],
        compiler_params=talk(0),
    )(tokens, cotangent, w1, table)

    hidden_part = compute(
        hidden_kernel, [SMEM, one_of((ROWS, WIDTH)), one_of(TILE)], whole(HIDDEN), shape(HIDDEN),
        [pltpu.VMEM(HIDDEN, f32)], tab_all, tok_all, w1_all,
    )

    w2_all, hidden_other = pl.pallas_call(
        second_kernel,
        out_shape=(shape((4,) + TILE), shape(HIDDEN)),
        in_specs=[ANY] * 2, out_specs=[ANY] * 2,
        scratch_shapes=[DMA((10,)), DMA((10,)), DMA((1,))],
        compiler_params=talk(1),
    )(w2, hidden_part)

    grad_part, out_part, second_part, slope = compute(
        forward_kernel,
        [SMEM, whole(HIDDEN), whole(HIDDEN), one_of((ROWS, WIDTH)), one_of(TILE)],
        [whole(HIDDEN), one_of((ROWS, WIDTH)), one_of(TILE), whole(HIDDEN)],
        (shape(HIDDEN), shape(MODEL), shape((4,) + TILE), shape(HIDDEN, f32)),
        [pltpu.VMEM(HIDDEN, bf16), pltpu.VMEM(HIDDEN, f32), pltpu.VMEM((ROWS, WIDTH), f32)],
        tab_all, hidden_part, hidden_other, cot_all, w2_all,
    )

    grad_other, second_grad, out_mid = pl.pallas_call(
        reduce_kernel,
        out_shape=(shape(HIDDEN), shape(TILE), shape((4, 64, WIDTH))),
        in_specs=[ANY, VMEM, VMEM], out_specs=[ANY, VMEM, VMEM],
        scratch_shapes=reduce_scratch() + [DMA((20,)), DMA((20,))],
        compiler_params=talk(2, 40),
    )(grad_part, second_part, out_part)

    in_part, first_part = compute(
        backward_kernel,
        [SMEM, whole(HIDDEN), whole(HIDDEN), whole(HIDDEN), one_of((ROWS, WIDTH)), one_of(TILE)],
        [one_of((ROWS, WIDTH)), one_of(TILE)],
        (shape(MODEL), shape((4,) + TILE)),
        [pltpu.VMEM(HIDDEN, bf16), pltpu.VMEM((ROWS, WIDTH), f32)],
        tab_all, grad_part, grad_other, slope, tok_all, w1_all,
    )

    first_grad, output, input_grad = pl.pallas_call(
        last_kernel,
        out_shape=(shape(TILE), shape((128, WIDTH)), shape((128, WIDTH))),
        in_specs=[VMEM] * 3, out_specs=[VMEM, ANY, ANY],
        scratch_shapes=reduce_scratch()
        + [pltpu.VMEM((4, 64, WIDTH), bf16)] + [pltpu.VMEM((4, 32, WIDTH), bf16)] * 2
        + [DMA((24,)), DMA((24,)), DMA((2,))],
        compiler_params=talk(3, 40),
    )(first_part, in_part, out_mid)
    return (output, input_grad, first_grad[None, None], second_grad[None, None])


def solution(mesh):
    return jax.shard_map(
        per_device,
        mesh=mesh,
        in_specs=(
            P("col", "row"),
            P("row", "col", None, None, None),
            P("col", "row", None, None, None),
            P("row", "col", None),
            P("row", "col"),
            P("col", "row"),
        ),
        out_specs=(
            P("col", "row"),
            P("col", "row"),
            P("row", "col", None, None, None),
            P("col", "row", None, None, None),
        ),
        check_vma=False,
    )
```

```python
import functools
import math

import jax
import jax.numpy as jnp
from jax import lax
from jax.experimental import pallas as pl
from jax.experimental.pallas import tpu as pltpu
from jax.sharding import PartitionSpec as P

BLK = 256
SLOTS = 8
HIDDEN_BLOCKS = 8
QUARTER = 32
WIDTH = 1024
ROWS = 512
bf16 = jnp.bfloat16
f32 = jnp.float32

gelu_scale = math.sqrt(2.0 / math.pi)
gelu_cubic = 0.044715
MIB = 1 << 20


def gelu_pair(hidden):
    inner = gelu_scale * (hidden + gelu_cubic * hidden * hidden * hidden)
    tanh_value = jnp.tanh(inner)
    value = 0.5 * hidden * (1.0 + tanh_value)
    slope = 0.5 * (1.0 + tanh_value) + 0.5 * hidden * (
        1.0 - tanh_value * tanh_value
    ) * gelu_scale * (1.0 + 3.0 * gelu_cubic * hidden * hidden)
    return (value, slope)


def y_index():
    return lax.div(lax.axis_index("row"), 2)


def peer(dx=0, dy=0, zl=0, zh=0, core=0):
    k, j = lax.axis_index("row"), lax.axis_index("col")
    row = lax.rem(lax.div(k, 2) + dy, 4) * 2 + lax.rem(lax.rem(k, 2) + zl, 2)
    col = (
        lax.rem(lax.div(j, 4) + dx, 4) * 4
        + lax.rem(lax.rem(lax.div(j, 2), 2) + zh, 2) * 2
        + lax.rem(lax.rem(j, 2) + core, 2)
    )
    return (row, col)


Y_PEERS = [dict(dy=1), dict(dy=2), dict(dy=3)]
X_PEERS = [dict(dx=1), dict(dx=3)]
CORE_PEER, ZH_PEER, ZL_PEER = dict(core=1), dict(zh=1), dict(zl=1)


def greet(peers):
    barrier = pltpu.get_barrier_semaphore()
    for one in peers:
        pl.semaphore_signal(barrier, inc=1, device_id=peer(**one), device_id_type=pl.DeviceIdType.MESH)
    pl.semaphore_wait(barrier, len(peers))


class Copies:
    def __init__(self, send, recv):
        self.send, self.recv, self.made, self.done = send, recv, [], set()

    def start(self, src, dst, **to):
        n = len(self.made)
        copy = pltpu.make_async_remote_copy(
            src_ref=src, dst_ref=dst, send_sem=self.send.at[n], recv_sem=self.recv.at[n],
            device_id=peer(**to), device_id_type=pl.DeviceIdType.MESH,
        )
        copy.start()
        self.made.append(copy)
        return copy

    def sent(self, *some):
        for copy in some:
            copy.wait_send()
            self.done.add(id(copy))

    def finish(self):
        for copy in self.made:
            if id(copy) not in self.done:
                copy.wait_send()


def span(start, size):
    return pl.ds(start, size)


LO, HI = span(0, 4), span(4, 4)


class WeightGather:
    def __init__(self, copies, own, slots):
        self.copies, self.own, self.slots = copies, own, slots

    def start(self):
        begin, own, slots = self.copies.start, self.own, self.slots
        self.up_lo = begin(own.at[LO], slots[3].at[LO], dy=1)
        self.down_hi = begin(own.at[HI], slots[1].at[HI], dy=3)
        self.up_hi = begin(own.at[HI], slots[3].at[HI], dy=1)
        self.down_lo = begin(own.at[LO], slots[1].at[LO], dy=3)

    def forward(self):
        self.up_lo.wait_recv()
        self.on_up = self.copies.start(self.slots[3].at[LO], self.slots[2].at[LO], dy=1)
        self.down_hi.wait_recv()
        self.on_down = self.copies.start(self.slots[1].at[HI], self.slots[2].at[HI], dy=3)

    def wait(self, r):
        for copy in {3: (self.up_hi,), 1: (self.down_lo,), 2: (self.on_up, self.on_down)}[r]:
            copy.wait_recv()


def part(core, x, zh, count=1):
    return (slice(None), slice(None), span(((core * 4 + x) * 2 + zh) * QUARTER, count * QUARTER))


def block(d):
    return span(d * BLK, BLK)


class RowGather:
    def __init__(self, copies, own, dest, local):
        self.copies, self.own, self.dest = copies, own, dest
        rows = pl.ds(pl.multiple_of(y_index() * QUARTER, QUARTER), QUARTER)
        self.mine = [
            pltpu.make_async_copy(own.at[rows, block(d)], dest.at[0, d, span(0, QUARTER)], local.at[d])
            for d in range(4)
        ]
        for copy in self.mine:
            copy.start()

    def spread(self):
        self.spread_copies = []
        for r in (1, 3, 2):
            rows = pl.ds(pl.multiple_of(lax.rem(y_index() + r, 4) * QUARTER, QUARTER), QUARTER)
            for d in range(4):
                self.spread_copies.append(self.copies.start(
                    self.own.at[rows, block(d)], self.dest.at[4 - r, d, span(0, QUARTER)], dy=r))

    def both_ways(self, zh):
        own = self.dest.at[part(0, 0, zh)]
        return (
            self.copies.start(own, self.dest.at[part(0, 3, zh)], dx=1),
            self.copies.start(own, self.dest.at[part(0, 1, zh)], dx=3),
        )

    def over(self, x):
        return self.copies.start(self.dest.at[part(0, x, 0, 2)], self.dest.at[part(1, x, 0, 2)], core=1)

    def across(self):
        for copy in self.mine:
            copy.wait()
        for copy in self.spread_copies:
            copy.wait_recv()
        self.across_copy = self.copies.start(self.dest.at[part(0, 0, 0)], self.dest.at[part(0, 0, 1)], zh=1)
        self.first = self.both_ways(0)

    def second(self):
        self.across_copy.wait_recv()
        self.next = self.both_ways(1)
        self.overs = [self.over(0)]

    def onward(self):
        self.first[0].wait_recv()
        self.on_up = self.copies.start(self.dest.at[part(0, 3, 0)], self.dest.at[part(0, 2, 0)], dx=1)
        self.next[1].wait_recv()
        self.on_down = self.copies.start(self.dest.at[part(0, 1, 1)], self.dest.at[part(0, 2, 1)], dx=3)

    def over_near(self):
        self.next[0].wait_recv()
        self.overs.append(self.over(3))
        self.first[1].wait_recv()
        self.overs.append(self.over(1))

    def over_far(self):
        self.on_up.wait_recv()
        self.on_down.wait_recv()
        self.overs.append(self.over(2))

    def finish(self):
        for copy in self.overs:
            copy.wait_recv()


def add_into(dst, *terms):
    def step(n, carry):
        total = terms[0][n].astype(f32)
        for term in terms[1:]:
            total = total + term[n].astype(f32)
        dst[n] = total.astype(dst.dtype)
        return carry

    lax.fori_loop(0, dst.shape[0], step, 0)


class RingReduce:
    def __init__(self, copies, part, far, near, axis):
        self.copies, self.part, self.far, self.near = copies, part, far, near
        self.up, self.down = {axis: 1}, {axis: 3}

    def start_far(self, h):
        way = (self.up, self.down)[h]
        copy = self.copies.start(self.part(2, h), self.far.at[h], **way)
        if h == 0:
            self.far_up = copy
        else:
            self.far_down = copy

    def start_near(self, h):
        if h == 0:
            self.near_up = self.copies.start(self.part(1, 1), self.near.at[0, 1], **self.up)
        else:
            self.near_down = self.copies.start(self.part(3, 0), self.near.at[1, 0], **self.down)

    def onward(self):
        self.far_up.wait_recv()
        add_into(self.far.at[0], self.far.at[0], self.part(1, 0))
        self.last_up = self.copies.start(self.far.at[0], self.near.at[0, 0], **self.up)
        self.far_down.wait_recv()
        add_into(self.far.at[1], self.far.at[1], self.part(3, 1))
        self.last_down = self.copies.start(self.far.at[1], self.near.at[1, 1], **self.down)

    def finish(self, dst):
        for copy in (self.near_up, self.near_down, self.last_up, self.last_down):
            copy.wait_recv()
        for h in range(2):
            add_into(dst(h), self.part(0, h), self.near.at[0, h], self.near.at[1, h])


def weight_part(partial):
    return lambda r, h: partial.at[r, (LO, HI)[h]]


class OutputReduce:
    def __init__(self, copies, partial, arrived, far, near):
        self.copies, self.partial, self.arrived, self.over = copies, partial, arrived, []
        self.ring = RingReduce(copies, lambda r, h: arrived.at[:, span(r * 64 + h * 32, 32)], far, near, "dx")

    def start(self, t):
        self.over.append(self.copies.start(self.partial.at[t, span(256, 256)], self.arrived.at[t], core=1))

    def join(self, r):
        rows = span(64 * r, 64)
        add_into(self.arrived.at[:, rows], self.arrived.at[:, rows], self.partial.at[:, rows])

    def begin_ring(self):
        for copy in self.over:
            copy.wait_recv()
        self.join(2)
        self.ring.start_far(0)
        self.ring.start_far(1)
        self.join(1)
        self.ring.start_near(0)
        self.join(3)
        self.ring.start_near(1)
        self.join(0)


class Home:
    def __init__(self, copies, mid, arrived, output, local):
        self.copies, self.mid, self.arrived, self.output, self.local = copies, mid, arrived, output, local

    def start(self):
        self.over = self.copies.start(self.mid.at[:, span(32, 32)], self.arrived, zh=1)

    def send(self):
        self.over.wait_recv()
        add_into(self.arrived, self.arrived, self.mid.at[:, span(0, 32)])
        rows = pl.ds(pl.multiple_of(y_index() * QUARTER, QUARTER), QUARTER)
        self.mine = pltpu.make_async_copy(self.arrived.at[0], self.output.at[rows], self.local)
        self.mine.start()
        self.sent = [self.copies.start(self.arrived.at[r], self.output.at[rows], dy=r) for r in (2, 1, 3)]

    def finish(self):
        self.mine.wait()
        for copy in self.sent:
            copy.wait_recv()


def columns(d):
    return pl.ds(pl.multiple_of(d * BLK, BLK), BLK)


def dot(a, b, da, db):
    return lax.dot_general(a, b, (((da,), (db,)), ((), ())), preferred_element_type=f32)


def tile_sum(rows, weights, tab, t, h, flipped):
    total = None
    for d in range(4):
        product = dot(rows[t, d], weights[t][tab[t, 0, d * HIDDEN_BLOCKS + h]], 1, int(flipped))
        total = product if total is None else total + product
    return total


def add_tile(rows, weights, tab, t, total, flipped, begin=False):
    def step(h, carry):
        if begin:
            total[h] = tile_sum(rows, weights, tab, t, h, flipped)
        else:
            total[h] += tile_sum(rows, weights, tab, t, h, flipped)
        return carry

    lax.fori_loop(0, HIDDEN_BLOCKS, step, 0)


def last_tile(rows, weights, tab, t, total, flipped, result, first, count):
    def step(h, carry):
        result[h] = (total[h] + tile_sum(rows, weights, tab, t, h, flipped)).astype(bf16)
        return carry

    lax.fori_loop(first, first + count, step, 0)


def model_tile(hidden, weights, tab, t, result, flipped):
    def step(d, carry):
        total = None
        for h in range(HIDDEN_BLOCKS):
            product = dot(hidden[h], weights[t][tab[t, 0, d * HIDDEN_BLOCKS + h]], 1, int(flipped))
            total = product if total is None else total + product
        result[t, :, columns(d)] = total.astype(bf16)
        return carry

    lax.fori_loop(0, 4, step, 0)


def slot_grads(tab, t, first, hidden, rows, result, hidden_left):
    def step(s, carry):
        live = tab[t, 0, 48 + s].astype(f32)
        left, right = hidden[tab[t, 0, 40 + s]], rows[t, tab[t, 0, 32 + s]]
        if not hidden_left:
            left, right = right, left
        result[t, s] = (dot(left, right, 0, 0) * live).astype(bf16)
        return carry

    lax.fori_loop(first, first + 4, step, 0)


CHUNK = 64
CHUNKS = ROWS // CHUNK


def over_chunks(first, count, work):
    def step(n, carry):
        work(first + lax.div(n, CHUNKS), pl.ds(pl.multiple_of(lax.rem(n, CHUNKS) * CHUNK, CHUNK), CHUNK))
        return carry

    lax.fori_loop(0, count * CHUNKS, step, 0)


def layer_kernel(tok, cot, w1, w2, tab_in, output, input_grad, first_grad, second_grad,
                 tok_all, cot_all, w1_0, w1_1, w1_2, w1_3, w2_0, w2_1, w2_2, w2_3,
                 total, hid, hid_other, grad, grad_other, act, model_part, second_part, first_part,
                 far_s, near_s, far_f, near_f, arrived_o, far_o, near_o, arrived_i, far_i, near_i,
                 mid_o, mid_i, home_o, home_i, tab_all, tab, send, recv, local):
    greet(Y_PEERS + X_PEERS + [CORE_PEER, ZH_PEER, ZL_PEER])
    copies = Copies(send, recv)
    first_w, second_w = (w1_0, w1_1, w1_2, w1_3), (w2_0, w2_1, w2_2, w2_3)
    tokens = RowGather(copies, tok, tok_all, local.at[span(14, 4)])
    tab_mine = pltpu.make_async_copy(tab_in, tab_all.at[0], local.at[1])
    tab_mine.start()
    w1_mine = pltpu.make_async_copy(w1, w1_0.at[span(0, SLOTS)], local.at[2])
    w1_mine.start()
    tokens.spread()
    tabs = [copies.start(tab_in, tab_all.at[4 - r], dy=r) for r in (1, 2, 3)]
    w1_ring = WeightGather(copies, w1, first_w)
    w1_ring.start()
    cotangent = RowGather(copies, cot, cot_all, local.at[span(10, 4)])
    w2_mine = pltpu.make_async_copy(w2, w2_0.at[span(0, SLOTS)], local.at[4])
    w2_mine.start()
    for weights in first_w + second_w:
        weights[SLOTS] = jnp.zeros((BLK, BLK), bf16)
    tokens.across()
    cotangent.spread()
    tokens.second()
    tokens.onward()
    w1_ring.forward()
    tokens.over_near()
    tokens.over_far()
    cotangent.across()
    for copy in tabs:
        copy.wait_recv()
    tab_mine.wait()
    tab_down = pltpu.make_async_copy(tab_all, tab, local.at[5])
    tab_down.start()
    tab_down.wait()
    tokens.finish()
    w1_mine.wait()

    add_tile(tok_all, first_w, tab, 0, total, False, True)
    cotangent.second()
    w1_ring.wait(3)
    add_tile(tok_all, first_w, tab, 3, total, False)
    w1_ring.wait(1)
    add_tile(tok_all, first_w, tab, 1, total, False)
    cotangent.onward()
    w1_ring.wait(2)
    w2_ring = WeightGather(copies, w2, second_w)
    w2_ring.start()
    swaps = []
    for n in range(4):
        last_tile(tok_all, first_w, tab, 2, total, False, hid, 2 * n, 2)
        pair = span(2 * n, 2)
        swaps.append(copies.start(hid.at[pair], hid_other.at[pair], zl=1))
    cotangent.over_near()
    cotangent.over_far()
    cotangent.finish()
    w2_mine.wait()

    add_tile(cot_all, second_w, tab, 0, total, True, True)
    w2_ring.forward()
    w2_ring.wait(3)
    add_tile(cot_all, second_w, tab, 3, total, True)
    w2_ring.wait(1)
    add_tile(cot_all, second_w, tab, 1, total, True)
    w2_ring.wait(2)
    last_tile(cot_all, second_w, tab, 2, total, True, grad, 0, HIDDEN_BLOCKS)

    def activate(h, rows):
        value, slope = gelu_pair(hid[h, rows].astype(f32) + hid_other[h, rows].astype(f32))
        act[h, rows] = value.astype(bf16)
        total[h, rows] = slope

    back = []
    for n in range(4):
        swaps[n].wait_recv()
        for m in {2: (0,), 3: (1, 2, 3)}.get(n, ()):
            pair = span(2 * m, 2)
            back.append(copies.start(grad.at[pair], grad_other.at[pair], zl=1))
        over_chunks(2 * n, 2, activate)

    seconds = RingReduce(copies, weight_part(second_part), far_s, near_s, "dy")

    def make_second(t, first):
        slot_grads(tab, t, first, act, cot_all, second_part, True)

    def ring_of(ring, make):
        make(2, 0)
        ring.start_far(0)
        make(2, 4)
        ring.start_far(1)
        make(1, 4)
        ring.start_near(0)
        make(3, 0)
        ring.start_near(1)
        make(1, 0)
        make(3, 4)

    ring_of(seconds, make_second)
    outs = OutputReduce(copies, model_part, arrived_o, far_o, near_o)
    model_tile(act, second_w, tab, 0, model_part, False)
    outs.start(0)
    seconds.onward()
    for t in (1, 2, 3):
        model_tile(act, second_w, tab, t, model_part, False)
        outs.start(t)
    make_second(0, 0)
    make_second(0, 4)
    copies.sent(*swaps)

    def combine(h, rows):
        both = grad[h, rows].astype(f32) + grad_other[h, rows].astype(f32)
        hid[h, rows] = (both * total[h, rows]).astype(bf16)

    back[0].wait_recv()
    over_chunks(0, 2, combine)
    outs.begin_ring()
    back[1].wait_recv()
    over_chunks(2, 2, combine)
    outs.ring.onward()
    back[2].wait_recv()
    over_chunks(4, 2, combine)
    back[3].wait_recv()
    over_chunks(6, 2, combine)

    firsts = RingReduce(copies, weight_part(first_part), far_f, near_f, "dy")

    def make_first(t, first):
        slot_grads(tab, t, first, hid, tok_all, first_part, False)

    ring_of(firsts, make_first)
    outs.ring.finish(lambda h: mid_o.at[:, span(32 * h, 32)])
    out_home = Home(copies, mid_o, home_o, output, local.at[6])
    out_home.start()
    copies.sent(*outs.over)
    ins = OutputReduce(copies, model_part, arrived_i, far_i, near_i)
    model_tile(hid, first_w, tab, 0, model_part, True)
    ins.start(0)
    firsts.onward()
    out_home.send()
    for t in (1, 2, 3):
        model_tile(hid, first_w, tab, t, model_part, True)
        ins.start(t)
    seconds.finish(lambda h: second_part.at[0, (LO, HI)[h]])
    second_out = pltpu.make_async_copy(second_part.at[0], second_grad, local.at[7])
    second_out.start()
    ins.begin_ring()
    make_first(0, 0)
    make_first(0, 4)
    ins.ring.onward()
    ins.ring.finish(lambda h: mid_i.at[:, span(32 * h, 32)])
    in_home = Home(copies, mid_i, home_i, input_grad, local.at[8])
    in_home.start()
    in_home.send()
    firsts.finish(lambda h: first_part.at[0, (LO, HI)[h]])
    first_out = pltpu.make_async_copy(first_part.at[0], first_grad, local.at[9])
    first_out.start()
    out_home.finish()
    in_home.finish()
    second_out.wait()
    first_out.wait()
    copies.finish()


ANY = pl.BlockSpec(memory_space=pl.ANY)
HIDDEN = (HIDDEN_BLOCKS, ROWS, BLK)
TILE = (SLOTS, BLK, BLK)
MODEL = (4, ROWS, WIDTH)
DMA = pltpu.SemaphoreType.DMA


def vmem(*dims):
    return pltpu.VMEM(dims, bf16)


def table(block_places, counts):
    places, slots = block_places[0, 0], jnp.arange(SLOTS, dtype=jnp.int32)
    live = (slots < counts[0, 0]).astype(jnp.int32)
    here = (places[None, :] == jnp.arange(32, dtype=jnp.int32)[:, None]).astype(jnp.int32) * live[None, :]
    source = SLOTS + jnp.sum(here * (slots[None, :] - SLOTS), axis=1)
    row = jnp.concatenate(
        [source, places // HIDDEN_BLOCKS, places % HIDDEN_BLOCKS, live, jnp.zeros((128 - 56,), jnp.int32)])
    return jnp.broadcast_to(row[None], (8, 128))


def per_device(tokens, w1_blocks, w2_blocks, block_places, counts, cotangent):
    weight_ring = [vmem(2, 4, BLK, BLK), vmem(2, 2, 4, BLK, BLK)]
    output_ring = [vmem(4, 256, WIDTH), vmem(2, 4, 32, WIDTH), vmem(2, 2, 4, 32, WIDTH)]
    output, input_grad, first_grad, second_grad = pl.pallas_call(
        layer_kernel,
        out_shape=[jax.ShapeDtypeStruct(dims, bf16) for dims in ((128, WIDTH), (128, WIDTH), TILE, TILE)],
        in_specs=[ANY] * 5,
        out_specs=[ANY] * 4,
        scratch_shapes=[vmem(4, 4, ROWS, BLK)] * 2
        + [vmem(SLOTS + 1, BLK, BLK)] * 8
        + [pltpu.VMEM(HIDDEN, f32)] + [vmem(*HIDDEN)] * 5
        + [vmem(*MODEL)] + [vmem(4, *TILE)] * 2
        + weight_ring * 2 + output_ring * 2
        + [vmem(4, 64, WIDTH)] * 2 + [vmem(4, 32, WIDTH)] * 2
        + [pltpu.VMEM((4, 8, 128), jnp.int32), pltpu.SMEM((4, 8, 128), jnp.int32)]
        + [DMA((120,)), DMA((120,)), DMA((18,))],
        compiler_params=pltpu.CompilerParams(
            collective_id=0, has_side_effects=True, vmem_limit_bytes=62 * MIB),
    )(tokens, cotangent, w1_blocks[0, 0], w2_blocks[0, 0], table(block_places, counts))
    return (output, input_grad, first_grad[None, None], second_grad[None, None])


def solution(mesh):
    return jax.shard_map(
        per_device,
        mesh=mesh,
        in_specs=(
            P("col", "row"),
            P("row", "col", None, None, None),
            P("col", "row", None, None, None),
            P("row", "col", None),
            P("row", "col"),
            P("col", "row"),
        ),
        out_specs=(
            P("col", "row"),
            P("col", "row"),
            P("row", "col", None, None, None),
            P("col", "row", None, None, None),
        ),
        check_vma=False,
    )
```

```python
import functools
import math

import jax
import jax.numpy as jnp
from jax import lax
from jax.experimental import pallas as pl
from jax.experimental.pallas import tpu as pltpu
from jax.sharding import PartitionSpec as P

BLK = 256
SLOTS = 8
HIDDEN_BLOCKS = 8
QUARTER = 32
WIDTH = 1024
ROWS = 512
bf16 = jnp.bfloat16
f32 = jnp.float32

gelu_scale = math.sqrt(2.0 / math.pi)
gelu_cubic = 0.044715
MIB = 1 << 20


def gelu_pair(hidden):
    inner = gelu_scale * (hidden + gelu_cubic * hidden * hidden * hidden)
    tanh_value = jnp.tanh(inner)
    value = 0.5 * hidden * (1.0 + tanh_value)
    slope = 0.5 * (1.0 + tanh_value) + 0.5 * hidden * (
        1.0 - tanh_value * tanh_value
    ) * gelu_scale * (1.0 + 3.0 * gelu_cubic * hidden * hidden)
    return (value, slope)


def y_index():
    return lax.div(lax.axis_index("row"), 2)


def peer(dx=0, dy=0, zl=0, zh=0, core=0):
    k, j = lax.axis_index("row"), lax.axis_index("col")
    row = lax.rem(lax.div(k, 2) + dy, 4) * 2 + lax.rem(lax.rem(k, 2) + zl, 2)
    col = (
        lax.rem(lax.div(j, 4) + dx, 4) * 4
        + lax.rem(lax.rem(lax.div(j, 2), 2) + zh, 2) * 2
        + lax.rem(lax.rem(j, 2) + core, 2)
    )
    return (row, col)


Y_PEERS = [dict(dy=1), dict(dy=2), dict(dy=3)]
X_PEERS = [dict(dx=1), dict(dx=3)]
CORE_PEER, ZH_PEER, ZL_PEER = dict(core=1), dict(zh=1), dict(zl=1)


def greet(peers):
    barrier = pltpu.get_barrier_semaphore()
    for one in peers:
        pl.semaphore_signal(barrier, inc=1, device_id=peer(**one), device_id_type=pl.DeviceIdType.MESH)
    pl.semaphore_wait(barrier, len(peers))


class Copies:
    def __init__(self, send, recv):
        self.send, self.recv, self.made, self.done = send, recv, [], set()

    def start(self, src, dst, **to):
        n = len(self.made)
        copy = self.at(n, src, dst, **to)
        copy.start()
        self.made.append(copy)
        return copy

    def reserve(self, count):
        first = len(self.made)
        self.made += [None] * count
        return first

    def at(self, n, src, dst, **to):
        return pltpu.make_async_remote_copy(
            src_ref=src, dst_ref=dst, send_sem=self.send.at[n], recv_sem=self.recv.at[n],
            device_id=peer(**to), device_id_type=pl.DeviceIdType.MESH,
        )

    def sent(self, *some):
        for copy in some:
            copy.wait_send()
            self.done.add(id(copy))

    def finish(self):
        for copy in self.made:
            if copy is not None and id(copy) not in self.done:
                copy.wait_send()


def span(start, size):
    return pl.ds(start, size)


LO, HI = span(0, 4), span(4, 4)


class WeightGather:
    def __init__(self, copies, own, slots):
        self.copies, self.own, self.slots = copies, own, slots

    def start(self):
        begin, own, slots = self.copies.start, self.own, self.slots
        self.up_lo = begin(own.at[LO], slots[3].at[LO], dy=1)
        self.down_hi = begin(own.at[HI], slots[1].at[HI], dy=3)
        self.up_hi = begin(own.at[HI], slots[3].at[HI], dy=1)
        self.down_lo = begin(own.at[LO], slots[1].at[LO], dy=3)

    def forward(self):
        self.up_lo.wait_recv()
        self.on_up = self.copies.start(self.slots[3].at[LO], self.slots[2].at[LO], dy=1)
        self.down_hi.wait_recv()
        self.on_down = self.copies.start(self.slots[1].at[HI], self.slots[2].at[HI], dy=3)

    def wait(self, r):
        for copy in {3: (self.up_hi,), 1: (self.down_lo,), 2: (self.on_up, self.on_down)}[r]:
            copy.wait_recv()


def part(core, x, zh, count=1):
    return (slice(None), slice(None), span(((core * 4 + x) * 2 + zh) * QUARTER, count * QUARTER))


def block(d):
    return span(d * BLK, BLK)


class RowGather:
    def __init__(self, copies, own, dest, local, early=None):
        self.copies, self.own, self.dest, self.local, self.early = copies, own, dest, local, early
        self.overs = []
        if early is not None:
            self.early_copy = copies.start(own, early, zh=1)

    def spread(self):
        self.mine, self.spread_copies = [], []
        sources = [self.own]
        if self.early is not None:
            self.early_copy.wait_recv()
            sources.append(self.early)
        for r in (0, 1, 3, 2):
            rows = pl.ds(pl.multiple_of(lax.rem(y_index() + r, 4) * QUARTER, QUARTER), QUARTER)
            for zh, source in enumerate(sources):
                for d in range(4):
                    piece = source.at[rows, block(d)]
                    place = self.dest.at[(4 - r) % 4, d, span(zh * QUARTER, QUARTER)]
                    if r == 0:
                        copy = pltpu.make_async_copy(piece, place, self.local.at[len(self.mine)])
                        copy.start()
                        self.mine.append(copy)
                    else:
                        self.spread_copies.append(self.copies.start(piece, place, dy=r))

    def wait_spread(self):
        for copy in self.mine:
            copy.wait()
        for copy in self.spread_copies:
            copy.wait_recv()

    def both_ways(self, zh):
        own = self.dest.at[part(0, 0, zh)]
        return (
            self.copies.start(own, self.dest.at[part(0, 3, zh)], dx=1),
            self.copies.start(own, self.dest.at[part(0, 1, zh)], dx=3),
        )

    def over(self, x):
        self.overs.append(
            self.copies.start(self.dest.at[part(0, x, 0, 2)], self.dest.at[part(1, x, 0, 2)], core=1))

    def begin(self):
        self.wait_spread()
        if self.early is None:
            self.across = self.copies.start(self.dest.at[part(0, 0, 0)], self.dest.at[part(0, 0, 1)], zh=1)
            self.first = self.both_ways(0)
        else:
            up_0, down_0 = self.both_ways(0)
            up_1, down_1 = self.both_ways(1)
            self.first, self.next = (up_0, down_0), (up_1, down_1)
            self.over(0)

    def onward_up(self):
        self.first[0].wait_recv()
        self.on_up = self.copies.start(self.dest.at[part(0, 3, 0)], self.dest.at[part(0, 2, 0)], dx=1)

    def second(self):
        self.across.wait_recv()
        self.next = self.both_ways(1)
        self.over(0)

    def onward_down(self):
        self.next[1].wait_recv()
        self.on_down = self.copies.start(self.dest.at[part(0, 1, 1)], self.dest.at[part(0, 2, 1)], dx=3)

    def over_near(self):
        self.next[0].wait_recv()
        self.over(3)
        self.first[1].wait_recv()
        self.over(1)

    def over_far(self):
        self.on_up.wait_recv()
        self.on_down.wait_recv()
        self.over(2)

    def finish(self):
        for copy in self.overs:
            copy.wait_recv()


def add_into(dst, *terms):
    def add(*refs):
        total = refs[1][...].astype(f32)
        for ref in refs[2:]:
            total = total + ref[...].astype(f32)
        refs[0][...] = total.astype(dst.dtype)

    if len(dst.shape) == 2:
        add(dst, *terms)
    else:

        def step(n, carry):
            add(*[ref.at[n] for ref in (dst,) + terms])
            return carry

        lax.fori_loop(0, dst.shape[0], step, 0)


class RingReduce:
    def __init__(self, copies, part, far, near, axis):
        self.copies, self.part, self.far, self.near = copies, part, far, near
        self.up, self.down = {axis: 1}, {axis: 3}

    def start_far(self):
        self.far_up = self.copies.start(self.part(2, 0), self.far.at[0], **self.up)
        self.far_down = self.copies.start(self.part(2, 1), self.far.at[1], **self.down)

    def start_up(self):
        self.near_up = self.copies.start(self.part(1, 1), self.near.at[0, 1], **self.up)

    def start_down(self):
        self.near_down = self.copies.start(self.part(3, 0), self.near.at[1, 0], **self.down)

    def onward(self):
        self.far_up.wait_recv()
        add_into(self.far.at[0], self.far.at[0], self.part(1, 0))
        self.last_up = self.copies.start(self.far.at[0], self.near.at[0, 0], **self.up)
        self.far_down.wait_recv()
        add_into(self.far.at[1], self.far.at[1], self.part(3, 1))
        self.last_down = self.copies.start(self.far.at[1], self.near.at[1, 1], **self.down)

    def finish(self, dst):
        for h, arrivals in enumerate(((self.near_down, self.last_up), (self.near_up, self.last_down))):
            for copy in arrivals:
                copy.wait_recv()
            add_into(dst(h), self.part(0, h), self.near.at[0, h], self.near.at[1, h])


def weight_part(partial):
    return lambda r, h: partial.at[r, (LO, HI)[h]]


class OutputReduce:
    def __init__(self, copies, t, partial, arrived, far, near, mid, home):
        self.copies, self.t, self.partial, self.arrived, self.mid, self.home = copies, t, partial, arrived, mid, home
        self.ring = RingReduce(copies, lambda r, h: arrived.at[span(r * 64 + h * 32, 32)], far, near, "dx")

    def start(self):
        self.over = self.copies.start(self.partial.at[span(256, 256)], self.arrived, core=1)

    def join(self, r):
        rows = span(64 * r, 64)
        add_into(self.arrived.at[rows], self.arrived.at[rows], self.partial.at[rows])

    def begin(self):
        self.over.wait_recv()
        self.join(2)
        self.ring.start_far()
        self.join(1)
        self.ring.start_up()
        self.join(3)
        self.ring.start_down()
        self.join(0)

    def finish(self):
        self.ring.finish(lambda h: self.mid.at[span(32 * h, 32)])

    def across(self):
        self.across_copy = self.copies.start(self.mid.at[span(32, 32)], self.home, zh=1)

    def send_home(self, output, local):
        self.across_copy.wait_recv()
        add_into(self.home, self.home, self.mid.at[span(0, 32)])
        rows = pl.ds(pl.multiple_of(y_index() * QUARTER, QUARTER), QUARTER)
        if self.t == 0:
            self.last = pltpu.make_async_copy(self.home, output.at[rows], local)
            self.last.start()
        else:
            self.last = self.copies.start(self.home, output.at[rows], dy=self.t)

    def arrive(self):
        if self.t == 0:
            self.last.wait()
        else:
            self.last.wait_recv()


def columns(d):
    return pl.ds(pl.multiple_of(d * BLK, BLK), BLK)


def dot(a, b, da, db):
    return lax.dot_general(a, b, (((da,), (db,)), ((), ())), preferred_element_type=f32)


def hidden_block(rows, weights, tab, h, flipped):
    total = None
    for t in range(4):
        for d in range(4):
            weight = weights[t][tab[t, 0, d * HIDDEN_BLOCKS + h]]
            product = dot(rows[t, d], weight, 1, int(flipped))
            total = product if total is None else total + product
    return total.astype(bf16)


def model_tile(hidden, weights, tab, t, result, flipped, blocks, add=False):
    def step(n, carry):
        for d in (2 * n, 2 * n + 1):
            total = result[t, :, columns(d)].astype(f32) if add else None
            for h in blocks:
                product = dot(hidden[h], weights[t][tab[t, 0, d * HIDDEN_BLOCKS + h]], 1, int(flipped))
                total = product if total is None else total + product
            result[t, :, columns(d)] = total.astype(bf16)
        return carry

    lax.fori_loop(0, 2, step, 0)


def slot_grads(tab, t, hidden, rows, result, hidden_left):
    for s in range(SLOTS):
        live = tab[t, 0, 48 + s].astype(f32)
        left, right = hidden[tab[t, 0, 40 + s]], rows[t, tab[t, 0, 32 + s]]
        if not hidden_left:
            left, right = right, left
        result[t, s] = (dot(left, right, 0, 0) * live).astype(bf16)


CHUNK = 64
CHUNKS = ROWS // CHUNK


def over_chunks(h, work):
    def step(n, carry):
        work(h, pl.ds(pl.multiple_of(n * CHUNK, CHUNK), CHUNK))
        return carry

    lax.fori_loop(0, CHUNKS, step, 0)


def layer_kernel(tok, cot, w1, w2, tab_in, output, input_grad, first_grad, second_grad,
                 tok_all, cot_all, w1_0, w1_1, w1_2, w1_3, w2_0, w2_1, w2_2, w2_3,
                 slope_all, hid, hid_other, grad, grad_other, act, model_part, second_part, first_part,
                 far_s, near_s, far_f, near_f, arrived_o, far_o, near_o, mid_o, home_o,
                 arrived_i, far_i, near_i, mid_i, home_i, cot_early, tab_all, tab, send, recv, local):
    greet(Y_PEERS + X_PEERS + [CORE_PEER, ZH_PEER, ZL_PEER])
    copies = Copies(send, recv)
    first_w, second_w = (w1_0, w1_1, w1_2, w1_3), (w2_0, w2_1, w2_2, w2_3)
    tokens = RowGather(copies, tok, tok_all, local.at[span(14, 4)])
    tokens.spread()
    w1_ring = WeightGather(copies, w1, first_w)
    w1_ring.start()
    tabs = [copies.start(tab_in, tab_all.at[4 - r], dy=r) for r in (1, 2, 3)]
    tab_mine = pltpu.make_async_copy(tab_in, tab_all.at[0], local.at[1])
    tab_mine.start()
    w1_mine = pltpu.make_async_copy(w1, w1_0.at[span(0, SLOTS)], local.at[2])
    w1_mine.start()
    w2_mine = pltpu.make_async_copy(w2, w2_0.at[span(0, SLOTS)], local.at[4])
    w2_mine.start()
    for weights in first_w + second_w:
        weights[SLOTS] = jnp.zeros((BLK, BLK), bf16)
    tokens.begin()
    tokens.onward_up()
    tokens.second()
    cotangent = RowGather(copies, cot, cot_all, local.at[span(18, 8)], cot_early)
    w1_ring.forward()
    tokens.onward_down()
    tokens.over_near()
    tokens.over_far()
    for copy in tabs:
        copy.wait_recv()
    tab_mine.wait()
    tab_down = pltpu.make_async_copy(tab_all, tab, local.at[5])
    tab_down.start()
    tab_down.wait()
    tokens.finish()
    w1_mine.wait()
    for r in (3, 1, 2):
        w1_ring.wait(r)
    cotangent.spread()
    w2_ring = WeightGather(copies, w2, second_w)
    w2_ring.start()

    swap = copies.reserve(HIDDEN_BLOCKS)
    back = copies.reserve(HIDDEN_BLOCKS)

    def swap_copy(h):
        return copies.at(swap + h, hid.at[h], hid_other.at[h], zl=1)

    def back_copy(h):
        return copies.at(back + h, grad.at[h], grad_other.at[h], zl=1)

    def make_hidden(h, carry):
        hid[h] = hidden_block(tok_all, first_w, tab, h, False)
        swap_copy(h).start()
        return carry

    lax.fori_loop(0, 4, make_hidden, 0)
    cotangent.begin()
    lax.fori_loop(4, 8, make_hidden, 0)
    cotangent.onward_up()
    w2_ring.forward()
    cotangent.onward_down()

    def activate(h, rows):
        value, slope = gelu_pair(hid[h, rows].astype(f32) + hid_other[h, rows].astype(f32))
        act[h, rows] = value.astype(bf16)
        slope_all[h, rows] = slope

    def activations(*blocks):
        for h in blocks:
            swap_copy(h).wait_recv()
            over_chunks(h, activate)

    activations(0, 1)
    cotangent.over_near()
    cotangent.over_far()
    activations(2, 3)
    cotangent.finish()
    w2_mine.wait()

    def make_grad(h, carry):
        grad[h] = hidden_block(cot_all, second_w, tab, h, True)
        return carry

    for r in (3, 1, 2):
        w2_ring.wait(r)
    lax.fori_loop(0, 4, make_grad, 0)
    activations(4, 5, 6)
    for h in range(4):
        back_copy(h).start()
    activations(7)

    seconds = RingReduce(copies, weight_part(second_part), far_s, near_s, "dy")

    def begin_ring(ring, hidden, rows, result, hidden_left):
        slot_grads(tab, 2, hidden, rows, result, hidden_left)
        ring.start_far()
        slot_grads(tab, 1, hidden, rows, result, hidden_left)
        ring.start_up()
        slot_grads(tab, 3, hidden, rows, result, hidden_left)
        ring.start_down()
        slot_grads(tab, 0, hidden, rows, result, hidden_left)

    def make_rest(h, carry):
        make_grad(h, carry)
        back_copy(h).start()
        return carry

    begin_ring(seconds, act, cot_all, second_part, True)
    lax.fori_loop(4, 8, make_rest, 0)
    order = (2, 1, 3, 0)
    every = tuple(range(HIDDEN_BLOCKS))
    outs = {t: OutputReduce(copies, t, model_part.at[t], arrived_o.at[t], far_o.at[t], near_o.at[t], mid_o.at[t], home_o.at[t])
            for t in order}
    for t in order:
        model_tile(act, second_w, tab, t, model_part, False, every)
        outs[t].start()
    seconds.onward()
    for h in range(HIDDEN_BLOCKS):
        swap_copy(h).wait_send()

    def combine(h, rows):
        both = grad[h, rows].astype(f32) + grad_other[h, rows].astype(f32)
        hid[h, rows] = (both * slope_all[h, rows]).astype(bf16)

    def combined(*blocks):
        for h in blocks:
            back_copy(h).wait_recv()
            over_chunks(h, combine)

    combined(0, 1)
    for t in order:
        outs[t].begin()
    combined(2, 3)
    for t in order:
        outs[t].ring.onward()
    combined(4, 5)

    copies.sent(*[outs[t].over for t in order])
    for t in order:
        model_tile(hid, first_w, tab, t, model_part, True, every[:6])
    combined(6, 7)
    firsts = RingReduce(copies, weight_part(first_part), far_f, near_f, "dy")
    ins = {t: OutputReduce(copies, t, model_part.at[t], arrived_i.at[t], far_i.at[t], near_i.at[t], mid_i.at[t], home_i.at[t])
           for t in order}
    begin_ring(firsts, hid, tok_all, first_part, False)
    for t in order:
        model_tile(hid, first_w, tab, t, model_part, True, every[6:], True)
        ins[t].start()
    for t in order:
        ins[t].begin()
    for t in order:
        outs[t].finish()
        outs[t].across()
    firsts.onward()
    for t in order:
        outs[t].send_home(output, local.at[6])
    for t in order:
        ins[t].ring.onward()
    seconds.finish(lambda h: second_part.at[0, (LO, HI)[h]])
    second_out = pltpu.make_async_copy(second_part.at[0], second_grad, local.at[7])
    second_out.start()
    for t in order:
        ins[t].finish()
        ins[t].across()
    for t in order:
        ins[t].send_home(input_grad, local.at[8])
    firsts.finish(lambda h: first_part.at[0, (LO, HI)[h]])
    first_out = pltpu.make_async_copy(first_part.at[0], first_grad, local.at[9])
    first_out.start()
    for t in order:
        outs[t].arrive()
        ins[t].arrive()
    second_out.wait()
    first_out.wait()
    for h in range(HIDDEN_BLOCKS):
        back_copy(h).wait_send()
    copies.finish()


def place_kernel(*refs):
    for source, dest in zip(refs[:4], refs[4:]):
        dest[...] = source[...]


ANY = pl.BlockSpec(memory_space=pl.ANY)
HIDDEN = (HIDDEN_BLOCKS, ROWS, BLK)
TILE = (SLOTS, BLK, BLK)
MODEL = (4, ROWS, WIDTH)
DMA = pltpu.SemaphoreType.DMA


def vmem(*dims):
    return pltpu.VMEM(dims, bf16)


def table(block_places, counts):
    places, slots = block_places[0, 0], jnp.arange(SLOTS, dtype=jnp.int32)
    live = (slots < counts[0, 0]).astype(jnp.int32)
    here = (places[None, :] == jnp.arange(32, dtype=jnp.int32)[:, None]).astype(jnp.int32) * live[None, :]
    source = SLOTS + jnp.sum(here * (slots[None, :] - SLOTS), axis=1)
    row = jnp.concatenate(
        [source, places // HIDDEN_BLOCKS, places % HIDDEN_BLOCKS, live, jnp.zeros((128 - 56,), jnp.int32)])
    return jnp.broadcast_to(row[None], (8, 128))


def per_device(tokens, w1_blocks, w2_blocks, block_places, counts, cotangent):
    weight_ring = [vmem(2, 4, BLK, BLK), vmem(2, 2, 4, BLK, BLK)]
    output_ring = [vmem(4, 256, WIDTH), vmem(4, 2, 32, WIDTH), vmem(4, 2, 2, 32, WIDTH), vmem(4, 64, WIDTH), vmem(4, 32, WIDTH)]
    shapes = [jax.ShapeDtypeStruct(dims, bf16) for dims in ((128, WIDTH), (128, WIDTH), TILE, TILE)]
    results = pl.pallas_call(
        layer_kernel,
        out_shape=shapes,
        in_specs=[ANY] * 5,
        out_specs=[ANY] * 4,
        scratch_shapes=[vmem(4, 4, ROWS, BLK)] * 2
        + [vmem(SLOTS + 1, BLK, BLK)] * 8
        + [pltpu.VMEM(HIDDEN, f32)] + [vmem(*HIDDEN)] * 5
        + [vmem(*MODEL)] + [vmem(4, *TILE)] * 2
        + weight_ring * 2 + output_ring * 2
        + [vmem(128, WIDTH)]
        + [pltpu.VMEM((4, 8, 128), jnp.int32), pltpu.SMEM((4, 8, 128), jnp.int32)]
        + [DMA((200,)), DMA((200,)), DMA((26,))],
        compiler_params=pltpu.CompilerParams(
            collective_id=0, has_side_effects=True, vmem_limit_bytes=62 * MIB),
    )(tokens, cotangent, w1_blocks[0, 0], w2_blocks[0, 0], table(block_places, counts))
    blocks = [pl.BlockSpec((32, WIDTH), lambda n: (n, 0))] * 2 + [pl.BlockSpec((2, BLK, BLK), lambda n: (n, 0, 0))] * 2
    output, input_grad, first_grad, second_grad = pl.pallas_call(
        place_kernel, grid=(4,), out_shape=shapes, in_specs=blocks, out_specs=blocks,
    )(*results)
    return (output, input_grad, first_grad[None, None], second_grad[None, None])


def solution(mesh):
    return jax.shard_map(
        per_device,
        mesh=mesh,
        in_specs=(
            P("col", "row"),
            P("row", "col", None, None, None),
            P("col", "row", None, None, None),
            P("row", "col", None),
            P("row", "col"),
            P("col", "row"),
        ),
        out_specs=(
            P("col", "row"),
            P("col", "row"),
            P("row", "col", None, None, None),
            P("col", "row", None, None, None),
        ),
        check_vma=False,
    )
```

```python
import functools
import math

import jax
import jax.numpy as jnp
from jax import lax
from jax.experimental import pallas as pl
from jax.experimental.pallas import tpu as pltpu
from jax.sharding import PartitionSpec as P

BLK = 256
SLOTS = 8
HIDDEN_BLOCKS = 8
QUARTER = 32
WIDTH = 1024
ROWS = 512
bf16 = jnp.bfloat16
f32 = jnp.float32

gelu_scale = math.sqrt(2.0 / math.pi)
gelu_cubic = 0.044715
MIB = 1 << 20


def gelu_pair(hidden):
    inner = gelu_scale * (hidden + gelu_cubic * hidden * hidden * hidden)
    tanh_value = jnp.tanh(inner)
    value = 0.5 * hidden * (1.0 + tanh_value)
    slope = 0.5 * (1.0 + tanh_value) + 0.5 * hidden * (
        1.0 - tanh_value * tanh_value
    ) * gelu_scale * (1.0 + 3.0 * gelu_cubic * hidden * hidden)
    return (value, slope)


def y_index():
    return lax.div(lax.axis_index("row"), 2)


def peer(dx=0, dy=0, zl=0, zh=0, core=0):
    k, j = lax.axis_index("row"), lax.axis_index("col")
    row = lax.rem(lax.div(k, 2) + dy, 4) * 2 + lax.rem(lax.rem(k, 2) + zl, 2)
    col = (
        lax.rem(lax.div(j, 4) + dx, 4) * 4
        + lax.rem(lax.rem(lax.div(j, 2), 2) + zh, 2) * 2
        + lax.rem(lax.rem(j, 2) + core, 2)
    )
    return (row, col)


Y_PEERS = [dict(dy=1), dict(dy=2), dict(dy=3)]
X_PEERS = [dict(dx=1), dict(dx=3)]
CORE_PEER, ZH_PEER, ZL_PEER = dict(core=1), dict(zh=1), dict(zl=1)


def greet(peers):
    barrier = pltpu.get_barrier_semaphore()
    for one in peers:
        pl.semaphore_signal(barrier, inc=1, device_id=peer(**one), device_id_type=pl.DeviceIdType.MESH)
    pl.semaphore_wait(barrier, len(peers))


class Copies:
    def __init__(self, send, recv):
        self.send, self.recv, self.made, self.done = send, recv, [], set()

    def make(self, src, dst, **to):
        copy = self.at(len(self.made), src, dst, **to)
        self.made.append(copy)
        return copy

    def start(self, src, dst, **to):
        copy = self.make(src, dst, **to)
        copy.start()
        return copy

    def reserve(self, count):
        first = len(self.made)
        self.made += [None] * count
        return first

    def at(self, n, src, dst, **to):
        return pltpu.make_async_remote_copy(
            src_ref=src, dst_ref=dst, send_sem=self.send.at[n], recv_sem=self.recv.at[n],
            device_id=peer(**to), device_id_type=pl.DeviceIdType.MESH,
        )

    def sent(self, *some):
        for copy in some:
            copy.wait_send()
            self.done.add(id(copy))

    def finish(self):
        for copy in self.made:
            if copy is not None and id(copy) not in self.done:
                copy.wait_send()


def span(start, size):
    return pl.ds(start, size)


LO, HI = span(0, 4), span(4, 4)


class WeightGather:
    def __init__(self, copies, own, slots):
        make = copies.make
        self.up_lo = make(own.at[LO], slots[3].at[LO], dy=1)
        self.down_hi = make(own.at[HI], slots[1].at[HI], dy=3)
        self.up_hi = make(own.at[HI], slots[3].at[HI], dy=1)
        self.down_lo = make(own.at[LO], slots[1].at[LO], dy=3)
        self.on_up = make(slots[3].at[LO], slots[2].at[LO], dy=1)
        self.on_down = make(slots[1].at[HI], slots[2].at[HI], dy=3)

    def start(self):
        for copy in (self.up_lo, self.down_hi, self.up_hi, self.down_lo):
            copy.start()

    def forward(self):
        self.up_lo.wait_recv()
        self.on_up.start()
        self.down_hi.wait_recv()
        self.on_down.start()

    def wait(self, r):
        for copy in {3: (self.up_hi,), 1: (self.down_lo,), 2: (self.on_up, self.on_down)}[r]:
            copy.wait_recv()


def part(core, x, zh, count=1):
    return (slice(None), slice(None), span(((core * 4 + x) * 2 + zh) * QUARTER, count * QUARTER))


def block(d):
    return span(d * BLK, BLK)


class RowGather:
    def __init__(self, copies, own, dest, local, early=None):
        self.copies, self.own, self.dest, self.local, self.early = copies, own, dest, local, early
        self.overs = []
        if early is not None:
            self.early_copy = copies.start(own, early, zh=1)

    def spread(self):
        self.mine, self.spread_copies = [], []
        sources = [self.own]
        if self.early is not None:
            self.early_copy.wait_recv()
            sources.append(self.early)
        for r in (0, 1, 3, 2):
            rows = pl.ds(pl.multiple_of(lax.rem(y_index() + r, 4) * QUARTER, QUARTER), QUARTER)
            for zh, source in enumerate(sources):
                for d in range(4):
                    piece = source.at[rows, block(d)]
                    place = self.dest.at[(4 - r) % 4, d, span(zh * QUARTER, QUARTER)]
                    if r == 0:
                        copy = pltpu.make_async_copy(piece, place, self.local.at[len(self.mine)])
                        copy.start()
                        self.mine.append(copy)
                    else:
                        self.spread_copies.append(self.copies.start(piece, place, dy=r))

    def wait_spread(self):
        for copy in self.mine:
            copy.wait()
        for copy in self.spread_copies:
            copy.wait_recv()

    def both_ways(self, zh):
        own = self.dest.at[part(0, 0, zh)]
        return (
            self.copies.start(own, self.dest.at[part(0, 3, zh)], dx=1),
            self.copies.start(own, self.dest.at[part(0, 1, zh)], dx=3),
        )

    def over(self, x):
        self.overs.append(
            self.copies.start(self.dest.at[part(0, x, 0, 2)], self.dest.at[part(1, x, 0, 2)], core=1))

    def begin(self):
        self.wait_spread()
        if self.early is None:
            self.across = self.copies.start(self.dest.at[part(0, 0, 0)], self.dest.at[part(0, 0, 1)], zh=1)
            self.first = self.both_ways(0)
        else:
            up_0, down_0 = self.both_ways(0)
            up_1, down_1 = self.both_ways(1)
            self.first, self.next = (up_0, down_0), (up_1, down_1)
            self.over(0)

    def onward_up(self):
        self.first[0].wait_recv()
        self.on_up = self.copies.start(self.dest.at[part(0, 3, 0)], self.dest.at[part(0, 2, 0)], dx=1)

    def second(self):
        self.across.wait_recv()
        self.next = self.both_ways(1)
        self.over(0)

    def onward_down(self):
        self.next[1].wait_recv()
        self.on_down = self.copies.start(self.dest.at[part(0, 1, 1)], self.dest.at[part(0, 2, 1)], dx=3)

    def over_near(self):
        self.next[0].wait_recv()
        self.over(3)
        self.first[1].wait_recv()
        self.over(1)

    def over_far(self):
        self.on_up.wait_recv()
        self.on_down.wait_recv()
        self.over(2)

    def finish(self):
        for copy in self.overs:
            copy.wait_recv()


def add_into(dst, *terms):
    def add(*refs):
        total = refs[1][...].astype(f32)
        for ref in refs[2:]:
            total = total + ref[...].astype(f32)
        refs[0][...] = total.astype(dst.dtype)

    if len(dst.shape) == 2:
        add(dst, *terms)
    else:

        def step(n, carry):
            add(*[ref.at[n] for ref in (dst,) + terms])
            return carry

        lax.fori_loop(0, dst.shape[0], step, 0)


class RingReduce:
    def __init__(self, copies, part, far, near, axis):
        self.copies, self.part, self.far, self.near = copies, part, far, near
        self.up, self.down = {axis: 1}, {axis: 3}

    def start_far(self):
        self.far_up = self.copies.start(self.part(2, 0), self.far.at[0], **self.up)
        self.far_down = self.copies.start(self.part(2, 1), self.far.at[1], **self.down)

    def start_up(self):
        self.near_up = self.copies.start(self.part(1, 1), self.near.at[0, 1], **self.up)

    def start_down(self):
        self.near_down = self.copies.start(self.part(3, 0), self.near.at[1, 0], **self.down)

    def onward(self):
        self.far_up.wait_recv()
        add_into(self.far.at[0], self.far.at[0], self.part(1, 0))
        self.last_up = self.copies.start(self.far.at[0], self.near.at[0, 0], **self.up)
        self.far_down.wait_recv()
        add_into(self.far.at[1], self.far.at[1], self.part(3, 1))
        self.last_down = self.copies.start(self.far.at[1], self.near.at[1, 1], **self.down)

    def finish(self, dst):
        for h, arrivals in enumerate(((self.near_down, self.last_up), (self.near_up, self.last_down))):
            for copy in arrivals:
                copy.wait_recv()
            add_into(dst(h), self.part(0, h), self.near.at[0, h], self.near.at[1, h])


def weight_part(partial):
    return lambda r, h: partial.at[r, (LO, HI)[h]]


class OutputReduce:
    def __init__(self, copies, t, partial, arrived, far, near, mid, home):
        self.copies, self.t, self.partial, self.arrived, self.mid, self.home = copies, t, partial, arrived, mid, home
        self.ring = RingReduce(copies, lambda r, h: arrived.at[span(r * 64 + h * 32, 32)], far, near, "dx")

    def start(self):
        self.over = self.copies.start(self.partial.at[span(256, 256)], self.arrived, core=1)

    def join(self, r):
        rows = span(64 * r, 64)
        add_into(self.arrived.at[rows], self.arrived.at[rows], self.partial.at[rows])

    def begin(self):
        self.over.wait_recv()
        self.join(2)
        self.ring.start_far()
        self.join(1)
        self.ring.start_up()
        self.join(3)
        self.ring.start_down()
        self.join(0)

    def finish(self):
        self.ring.finish(lambda h: self.mid.at[span(32 * h, 32)])

    def across(self):
        self.across_copy = self.copies.start(self.mid.at[span(32, 32)], self.home, zh=1)

    def send_home(self, output, local):
        self.across_copy.wait_recv()
        add_into(self.home, self.home, self.mid.at[span(0, 32)])
        rows = pl.ds(pl.multiple_of(y_index() * QUARTER, QUARTER), QUARTER)
        if self.t == 0:
            self.last = pltpu.make_async_copy(self.home, output.at[rows], local)
            self.last.start()
        else:
            self.last = self.copies.start(self.home, output.at[rows], dy=self.t)

    def arrive(self):
        if self.t == 0:
            self.last.wait()
        else:
            self.last.wait_recv()


def columns(d):
    return pl.ds(pl.multiple_of(d * BLK, BLK), BLK)


def dot(a, b, da, db):
    return lax.dot_general(a, b, (((da,), (db,)), ((), ())), preferred_element_type=f32)


def hidden_block(rows, weights, tab, h, flipped):
    total = None
    for t in range(4):
        for d in range(4):
            weight = weights[t][tab[t, 0, d * HIDDEN_BLOCKS + h]]
            product = dot(rows[t, d], weight, 1, int(flipped))
            total = product if total is None else total + product
    return total.astype(bf16)


def model_tile(hidden, weights, tab, t, result, flipped, blocks, add=False):
    def step(n, carry):
        for d in (2 * n, 2 * n + 1):
            total = result[t, :, columns(d)].astype(f32) if add else None
            for h in blocks:
                product = dot(hidden[h], weights[t][tab[t, 0, d * HIDDEN_BLOCKS + h]], 1, int(flipped))
                total = product if total is None else total + product
            result[t, :, columns(d)] = total.astype(bf16)
        return carry

    lax.fori_loop(0, 2, step, 0)


def slot_grads(tab, t, hidden, rows, result, hidden_left):
    for s in range(SLOTS):
        live = tab[t, 0, 48 + s].astype(f32)
        left, right = hidden[tab[t, 0, 40 + s]], rows[t, tab[t, 0, 32 + s]]
        if not hidden_left:
            left, right = right, left
        result[t, s] = (dot(left, right, 0, 0) * live).astype(bf16)


CHUNK = 64
CHUNKS = ROWS // CHUNK


def over_chunks(h, work):
    def step(n, carry):
        work(h, pl.ds(pl.multiple_of(n * CHUNK, CHUNK), CHUNK))
        return carry

    lax.fori_loop(0, CHUNKS, step, 0)


def layer_kernel(tok, cot, w1, w2, tab_in, output, input_grad, first_grad, second_grad,
                 tok_all, cot_all, w1_0, w1_1, w1_2, w1_3, w2_0, w2_1, w2_2, w2_3,
                 slope_all, hid, hid_other, grad, grad_other, act, model_part, second_part, first_part,
                 far_s, near_s, far_f, near_f, arrived_o, far_o, near_o, mid_o, home_o,
                 arrived_i, far_i, near_i, mid_i, home_i, cot_early, tab_all, tab, send, recv, local):
    greet(Y_PEERS + X_PEERS + [CORE_PEER, ZH_PEER, ZL_PEER])
    copies = Copies(send, recv)
    core = lax.rem(lax.axis_index("col"), 2)
    first_w, second_w = (w1_0, w1_1, w1_2, w1_3), (w2_0, w2_1, w2_2, w2_3)
    tokens = RowGather(copies, tok, tok_all, local.at[span(14, 4)])
    tokens.spread()
    w1_ring = WeightGather(copies, w1, first_w)
    on_first, on_second = pl.when(core == 0), pl.when(core == 1)
    on_first(w1_ring.start)
    tabs = [copies.start(tab_in, tab_all.at[4 - r], dy=r) for r in (1, 2, 3)]
    tab_mine = pltpu.make_async_copy(tab_in, tab_all.at[0], local.at[1])
    tab_mine.start()
    w1_mine = pltpu.make_async_copy(w1, w1_0.at[span(0, SLOTS)], local.at[2])
    w1_mine.start()
    w2_mine = pltpu.make_async_copy(w2, w2_0.at[span(0, SLOTS)], local.at[4])
    w2_mine.start()
    for weights in first_w + second_w:
        weights[SLOTS] = jnp.zeros((BLK, BLK), bf16)
    tokens.begin()
    tokens.onward_up()
    on_first(w1_ring.forward)
    tokens.second()
    on_second(w1_ring.start)
    cotangent = RowGather(copies, cot, cot_all, local.at[span(18, 8)], cot_early)
    tokens.onward_down()
    tokens.over_near()
    tokens.over_far()
    on_second(w1_ring.forward)
    for copy in tabs:
        copy.wait_recv()
    tab_mine.wait()
    tab_down = pltpu.make_async_copy(tab_all, tab, local.at[5])
    tab_down.start()
    tab_down.wait()
    tokens.finish()
    w1_mine.wait()
    for r in (3, 1, 2):
        w1_ring.wait(r)
    w2_ring = WeightGather(copies, w2, second_w)

    swap = copies.reserve(HIDDEN_BLOCKS)
    back = copies.reserve(HIDDEN_BLOCKS)

    def swap_copy(h):
        return copies.at(swap + h, hid.at[h], hid_other.at[h], zl=1)

    def back_copy(h):
        return copies.at(back + h, grad.at[h], grad_other.at[h], zl=1)

    def make_hidden(h, carry):
        hid[h] = hidden_block(tok_all, first_w, tab, h, False)
        swap_copy(h).start()
        return carry

    lax.fori_loop(0, 4, make_hidden, 0)
    cotangent.spread()
    w2_ring.start()
    cotangent.begin()
    lax.fori_loop(4, 8, make_hidden, 0)
    cotangent.onward_up()
    w2_ring.forward()
    cotangent.onward_down()

    def activate(h, rows):
        value, slope = gelu_pair(hid[h, rows].astype(f32) + hid_other[h, rows].astype(f32))
        act[h, rows] = value.astype(bf16)
        slope_all[h, rows] = slope

    def activations(*blocks):
        for h in blocks:
            swap_copy(h).wait_recv()
            over_chunks(h, activate)

    activations(0, 1)
    cotangent.over_near()
    cotangent.over_far()
    activations(2, 3)
    cotangent.finish()
    w2_mine.wait()

    def make_grad(h, carry):
        grad[h] = hidden_block(cot_all, second_w, tab, h, True)
        return carry

    for r in (3, 1, 2):
        w2_ring.wait(r)
    lax.fori_loop(0, 4, make_grad, 0)
    activations(4, 5, 6)
    for h in range(4):
        back_copy(h).start()
    activations(7)

    seconds = RingReduce(copies, weight_part(second_part), far_s, near_s, "dy")

    def begin_ring(ring, hidden, rows, result, hidden_left):
        slot_grads(tab, 2, hidden, rows, result, hidden_left)
        ring.start_far()
        slot_grads(tab, 1, hidden, rows, result, hidden_left)
        ring.start_up()
        slot_grads(tab, 3, hidden, rows, result, hidden_left)
        ring.start_down()
        slot_grads(tab, 0, hidden, rows, result, hidden_left)

    def make_rest(h, carry):
        make_grad(h, carry)
        back_copy(h).start()
        return carry

    begin_ring(seconds, act, cot_all, second_part, True)
    lax.fori_loop(4, 8, make_rest, 0)
    order = (2, 1, 3, 0)
    every = tuple(range(HIDDEN_BLOCKS))
    outs = {t: OutputReduce(copies, t, model_part.at[t], arrived_o.at[t], far_o.at[t], near_o.at[t], mid_o.at[t], home_o.at[t])
            for t in order}
    for t in order:
        model_tile(act, second_w, tab, t, model_part, False, every)
        outs[t].start()
    seconds.onward()
    for h in range(HIDDEN_BLOCKS):
        swap_copy(h).wait_send()

    def combine(h, rows):
        both = grad[h, rows].astype(f32) + grad_other[h, rows].astype(f32)
        hid[h, rows] = (both * slope_all[h, rows]).astype(bf16)

    def combined(*blocks):
        for h in blocks:
            back_copy(h).wait_recv()
            over_chunks(h, combine)

    combined(0, 1)
    for t in order:
        outs[t].begin()
    combined(2, 3)
    for t in order:
        outs[t].ring.onward()
    combined(4, 5)

    copies.sent(*[outs[t].over for t in order])
    for t in order:
        model_tile(hid, first_w, tab, t, model_part, True, every[:6])
    combined(6, 7)
    firsts = RingReduce(copies, weight_part(first_part), far_f, near_f, "dy")
    ins = {t: OutputReduce(copies, t, model_part.at[t], arrived_i.at[t], far_i.at[t], near_i.at[t], mid_i.at[t], home_i.at[t])
           for t in order}
    begin_ring(firsts, hid, tok_all, first_part, False)
    for t in order:
        model_tile(hid, first_w, tab, t, model_part, True, every[6:], True)
        ins[t].start()
    for t in order:
        ins[t].begin()
    for t in order:
        outs[t].finish()
        outs[t].across()
    firsts.onward()
    for t in order:
        outs[t].send_home(output, local.at[6])
    for t in order:
        ins[t].ring.onward()
    seconds.finish(lambda h: second_part.at[0, (LO, HI)[h]])
    second_out = pltpu.make_async_copy(second_part.at[0], second_grad, local.at[7])
    second_out.start()
    for t in order:
        ins[t].finish()
        ins[t].across()
    for t in order:
        ins[t].send_home(input_grad, local.at[8])
    firsts.finish(lambda h: first_part.at[0, (LO, HI)[h]])
    first_out = pltpu.make_async_copy(first_part.at[0], first_grad, local.at[9])
    first_out.start()
    for t in order:
        outs[t].arrive()
        ins[t].arrive()
    second_out.wait()
    first_out.wait()
    for h in range(HIDDEN_BLOCKS):
        back_copy(h).wait_send()
    copies.finish()


def place_kernel(*refs):
    for source, dest in zip(refs[:4], refs[4:]):
        dest[...] = source[...]


ANY = pl.BlockSpec(memory_space=pl.ANY)
HIDDEN = (HIDDEN_BLOCKS, ROWS, BLK)
TILE = (SLOTS, BLK, BLK)
MODEL = (4, ROWS, WIDTH)
DMA = pltpu.SemaphoreType.DMA


def vmem(*dims):
    return pltpu.VMEM(dims, bf16)


def table(block_places, counts):
    places, slots = block_places[0, 0], jnp.arange(SLOTS, dtype=jnp.int32)
    live = (slots < counts[0, 0]).astype(jnp.int32)
    here = (places[None, :] == jnp.arange(32, dtype=jnp.int32)[:, None]).astype(jnp.int32) * live[None, :]
    source = SLOTS + jnp.sum(here * (slots[None, :] - SLOTS), axis=1)
    row = jnp.concatenate(
        [source, places // HIDDEN_BLOCKS, places % HIDDEN_BLOCKS, live, jnp.zeros((128 - 56,), jnp.int32)])
    return jnp.broadcast_to(row[None], (8, 128))


def per_device(tokens, w1_blocks, w2_blocks, block_places, counts, cotangent):
    weight_ring = [vmem(2, 4, BLK, BLK), vmem(2, 2, 4, BLK, BLK)]
    output_ring = [vmem(4, 256, WIDTH), vmem(4, 2, 32, WIDTH), vmem(4, 2, 2, 32, WIDTH), vmem(4, 64, WIDTH), vmem(4, 32, WIDTH)]
    shapes = [jax.ShapeDtypeStruct(dims, bf16) for dims in ((128, WIDTH), (128, WIDTH), TILE, TILE)]
    results = pl.pallas_call(
        layer_kernel,
        out_shape=shapes,
        in_specs=[ANY] * 5,
        out_specs=[ANY] * 4,
        scratch_shapes=[vmem(4, 4, ROWS, BLK)] * 2
        + [vmem(SLOTS + 1, BLK, BLK)] * 8
        + [pltpu.VMEM(HIDDEN, f32)] + [vmem(*HIDDEN)] * 5
        + [vmem(*MODEL)] + [vmem(4, *TILE)] * 2
        + weight_ring * 2 + output_ring * 2
        + [vmem(128, WIDTH)]
        + [pltpu.VMEM((4, 8, 128), jnp.int32), pltpu.SMEM((4, 8, 128), jnp.int32)]
        + [DMA((200,)), DMA((200,)), DMA((26,))],
        compiler_params=pltpu.CompilerParams(
            collective_id=0, has_side_effects=True, vmem_limit_bytes=62 * MIB),
    )(tokens, cotangent, w1_blocks[0, 0], w2_blocks[0, 0], table(block_places, counts))
    blocks = [pl.BlockSpec((32, WIDTH), lambda n: (n, 0))] * 2 + [pl.BlockSpec((2, BLK, BLK), lambda n: (n, 0, 0))] * 2
    output, input_grad, first_grad, second_grad = pl.pallas_call(
        place_kernel, grid=(4,), out_shape=shapes, in_specs=blocks, out_specs=blocks,
    )(*results)
    return (output, input_grad, first_grad[None, None], second_grad[None, None])


def solution(mesh):
    return jax.shard_map(
        per_device,
        mesh=mesh,
        in_specs=(
            P("col", "row"),
            P("row", "col", None, None, None),
            P("col", "row", None, None, None),
            P("row", "col", None),
            P("row", "col"),
            P("col", "row"),
        ),
        out_specs=(
            P("col", "row"),
            P("col", "row"),
            P("row", "col", None, None, None),
            P("col", "row", None, None, None),
        ),
        check_vma=False,
    )
```

```python
import functools
import math

import jax
import jax.numpy as jnp
from jax import lax
from jax.experimental import pallas as pl
from jax.experimental.pallas import tpu as pltpu
from jax.sharding import PartitionSpec as P

BLK = 256
SLOTS = 8
HIDDEN_BLOCKS = 8
QUARTER = 32
WIDTH = 1024
ROWS = 512
bf16 = jnp.bfloat16
f32 = jnp.float32

gelu_scale = math.sqrt(2.0 / math.pi)
gelu_cubic = 0.044715
MIB = 1 << 20


def gelu_pair(hidden):
    inner = gelu_scale * (hidden + gelu_cubic * hidden * hidden * hidden)
    tanh_value = jnp.tanh(inner)
    value = 0.5 * hidden * (1.0 + tanh_value)
    slope = 0.5 * (1.0 + tanh_value) + 0.5 * hidden * (
        1.0 - tanh_value * tanh_value
    ) * gelu_scale * (1.0 + 3.0 * gelu_cubic * hidden * hidden)
    return (value, slope)


def y_index():
    return lax.div(lax.axis_index("row"), 2)


def peer(dx=0, dy=0, zl=0, zh=0, core=0):
    k, j = lax.axis_index("row"), lax.axis_index("col")
    row = lax.rem(lax.div(k, 2) + dy, 4) * 2 + lax.rem(lax.rem(k, 2) + zl, 2)
    col = (
        lax.rem(lax.div(j, 4) + dx, 4) * 4
        + lax.rem(lax.rem(lax.div(j, 2), 2) + zh, 2) * 2
        + lax.rem(lax.rem(j, 2) + core, 2)
    )
    return (row, col)


Y_PEERS = [dict(dy=1), dict(dy=2), dict(dy=3)]
X_PEERS = [dict(dx=1), dict(dx=3)]
CORE_PEER, ZH_PEER, ZL_PEER = dict(core=1), dict(zh=1), dict(zl=1)


def greet(peers):
    barrier = pltpu.get_barrier_semaphore()
    for one in peers:
        pl.semaphore_signal(barrier, inc=1, device_id=peer(**one), device_id_type=pl.DeviceIdType.MESH)
    pl.semaphore_wait(barrier, len(peers))


class Copies:
    def __init__(self, send, recv):
        self.send, self.recv, self.made, self.done = send, recv, [], set()

    def make(self, src, dst, **to):
        copy = self.at(len(self.made), src, dst, **to)
        self.made.append(copy)
        return copy

    def start(self, src, dst, **to):
        copy = self.make(src, dst, **to)
        copy.start()
        return copy

    def reserve(self, count):
        first = len(self.made)
        self.made += [None] * count
        return first

    def at(self, n, src, dst, **to):
        return pltpu.make_async_remote_copy(
            src_ref=src, dst_ref=dst, send_sem=self.send.at[n], recv_sem=self.recv.at[n],
            device_id=peer(**to), device_id_type=pl.DeviceIdType.MESH,
        )

    def sent(self, *some):
        for copy in some:
            copy.wait_send()
            self.done.add(id(copy))

    def finish(self):
        for copy in self.made:
            if copy is not None and id(copy) not in self.done:
                copy.wait_send()


def span(start, size):
    return pl.ds(start, size)


LO, HI = span(0, 4), span(4, 4)


class WeightGather:
    def __init__(self, copies, own, slots):
        make = copies.make
        self.up_lo = make(own.at[LO], slots[3].at[LO], dy=1)
        self.down_hi = make(own.at[HI], slots[1].at[HI], dy=3)
        self.up_hi = make(own.at[HI], slots[3].at[HI], dy=1)
        self.down_lo = make(own.at[LO], slots[1].at[LO], dy=3)
        self.on_up = make(slots[3].at[LO], slots[2].at[LO], dy=1)
        self.on_down = make(slots[1].at[HI], slots[2].at[HI], dy=3)

    def start(self):
        for copy in (self.up_lo, self.down_hi, self.up_hi, self.down_lo):
            copy.start()

    def forward(self):
        self.up_lo.wait_recv()
        self.on_up.start()
        self.down_hi.wait_recv()
        self.on_down.start()

    def wait(self, r):
        for copy in {3: (self.up_hi,), 1: (self.down_lo,), 2: (self.on_up, self.on_down)}[r]:
            copy.wait_recv()


def part(core, x, zh, count=1):
    return (slice(None), slice(None), span(((core * 4 + x) * 2 + zh) * QUARTER, count * QUARTER))


def block(d):
    return span(d * BLK, BLK)


class RowGather:
    def __init__(self, copies, own, dest, local):
        self.mine, self.spread_copies, make = [], [], copies.make
        for r in (0, 1, 3, 2):
            rows = pl.ds(pl.multiple_of(lax.rem(y_index() + r, 4) * QUARTER, QUARTER), QUARTER)
            for d in range(4):
                piece = own.at[rows, block(d)]
                place = dest.at[(4 - r) % 4, d, span(0, QUARTER)]
                if r == 0:
                    self.mine.append(pltpu.make_async_copy(piece, place, local.at[d]))
                else:
                    self.spread_copies.append(make(piece, place, dy=r))

        def both_ways(zh):
            held = dest.at[part(0, 0, zh)]
            return make(held, dest.at[part(0, 3, zh)], dx=1), make(held, dest.at[part(0, 1, zh)], dx=3)

        self.across = make(dest.at[part(0, 0, 0)], dest.at[part(0, 0, 1)], zh=1)
        self.first, self.next = both_ways(0), both_ways(1)
        self.on_up = make(dest.at[part(0, 3, 0)], dest.at[part(0, 2, 0)], dx=1)
        self.on_down = make(dest.at[part(0, 1, 1)], dest.at[part(0, 2, 1)], dx=3)
        self.over = [make(dest.at[part(0, x, 0, 2)], dest.at[part(1, x, 0, 2)], core=1) for x in range(4)]
        self.all = self.spread_copies + [self.across, *self.first, *self.next, self.on_up, self.on_down] + self.over

    def spread(self):
        for copy in self.mine + self.spread_copies:
            copy.start()

    def cross(self):
        for copy in self.mine:
            copy.wait()
        for copy in self.spread_copies:
            copy.wait_recv()
        self.across.start()

    def begin(self):
        for copy in self.first:
            copy.start()

    def onward_up(self):
        self.first[0].wait_recv()
        self.on_up.start()

    def second(self):
        self.across.wait_recv()
        for copy in self.next:
            copy.start()
        self.over[0].start()

    def onward_down(self):
        self.next[1].wait_recv()
        self.on_down.start()

    def over_near(self):
        self.next[0].wait_recv()
        self.over[3].start()
        self.first[1].wait_recv()
        self.over[1].start()

    def over_far(self):
        self.on_up.wait_recv()
        self.on_down.wait_recv()
        self.over[2].start()

    def finish(self):
        for copy in self.over:
            copy.wait_recv()


def add_into(dst, *terms):
    def add(*refs):
        total = refs[1][...].astype(f32)
        for ref in refs[2:]:
            total = total + ref[...].astype(f32)
        refs[0][...] = total.astype(dst.dtype)

    if len(dst.shape) == 2:
        add(dst, *terms)
    else:

        def step(n, carry):
            add(*[ref.at[n] for ref in (dst,) + terms])
            return carry

        lax.fori_loop(0, dst.shape[0], step, 0)


class RingReduce:
    def __init__(self, copies, part, far, near, axis):
        self.part, self.far, self.near = part, far, near
        up, down, make = {axis: 1}, {axis: 3}, copies.make
        self.far_up = make(part(2, 0), far.at[0], **up)
        self.far_down = make(part(2, 1), far.at[1], **down)
        self.near_up = make(part(1, 1), near.at[0, 1], **up)
        self.near_down = make(part(3, 0), near.at[1, 0], **down)
        self.last_up = make(far.at[0], near.at[0, 0], **up)
        self.last_down = make(far.at[1], near.at[1, 1], **down)

    def start_far(self):
        self.far_up.start()
        self.far_down.start()

    def start_up(self):
        self.near_up.start()

    def start_down(self):
        self.near_down.start()

    def onward(self):
        self.far_up.wait_recv()
        add_into(self.far.at[0], self.far.at[0], self.part(1, 0))
        self.last_up.start()
        self.far_down.wait_recv()
        add_into(self.far.at[1], self.far.at[1], self.part(3, 1))
        self.last_down.start()

    def finish(self, dst):
        for h, arrivals in enumerate(((self.near_down, self.last_up), (self.near_up, self.last_down))):
            for copy in arrivals:
                copy.wait_recv()
            for n in range(4):
                add_into(dst(h, n), self.part(0, h).at[n], self.near.at[0, h, n], self.near.at[1, h, n])


def weight_part(partial):
    return lambda r, h: partial.at[r, (LO, HI)[h]]


class OutputReduce:
    def __init__(self, copies, t, partial, arrived, far, near, mid, home):
        self.copies, self.t, self.partial, self.arrived, self.mid, self.home = copies, t, partial, arrived, mid, home
        self.ring = RingReduce(copies, lambda r, h: arrived.at[:, span(r * 64 + h * 32, 32)], far, near, "dx")

    def start(self):
        self.over = self.copies.start(self.partial.at[:, span(256, 256)], self.arrived, core=1)

    def join(self, r):
        rows = span(64 * r, 64)
        add_into(self.arrived.at[:, rows], self.arrived.at[:, rows], self.partial.at[:, rows])

    def begin(self):
        self.over.wait_recv()
        self.join(2)
        self.ring.start_far()
        self.join(1)
        self.ring.start_up()
        self.join(3)
        self.ring.start_down()
        self.join(0)

    def finish(self):
        self.ring.finish(lambda h, n: self.mid.at[span(32 * h, 32), block(n)])

    def across(self):
        self.across_copy = self.copies.start(self.mid.at[span(32, 32)], self.home, zh=1)

    def send_home(self, output, local):
        self.across_copy.wait_recv()
        add_into(self.home, self.home, self.mid.at[span(0, 32)])
        rows = pl.ds(pl.multiple_of(y_index() * QUARTER, QUARTER), QUARTER)
        if self.t == 0:
            self.last = pltpu.make_async_copy(self.home, output.at[rows], local)
            self.last.start()
        else:
            self.last = self.copies.start(self.home, output.at[rows], dy=self.t)

    def arrive(self):
        if self.t == 0:
            self.last.wait()
        else:
            self.last.wait_recv()


def dot(a, b, da, db):
    return lax.dot_general(a, b, (((da,), (db,)), ((), ())), preferred_element_type=f32)


def hidden_block(rows, weights, tab, h, flipped):
    total = None
    for t in range(4):
        for d in range(4):
            weight = weights[t][tab[t, 0, d * HIDDEN_BLOCKS + h]]
            product = dot(rows[t, d], weight, 1, int(flipped))
            total = product if total is None else total + product
    return total.astype(bf16)


def model_tile(hidden, weights, tab, t, result, flipped, blocks, add=False):
    def step(n, carry):
        for d in (2 * n, 2 * n + 1):
            total = result[t, d].astype(f32) if add else None
            for h in blocks:
                product = dot(hidden[h], weights[t][tab[t, 0, d * HIDDEN_BLOCKS + h]], 1, int(flipped))
                total = product if total is None else total + product
            result[t, d] = total.astype(bf16)
        return carry

    lax.fori_loop(0, 2, step, 0)


def slot_grads(tab, t, hidden, rows, result, hidden_left):
    for s in range(SLOTS):
        live = tab[t, 0, 48 + s].astype(f32)
        left, right = hidden[tab[t, 0, 40 + s]], rows[t, tab[t, 0, 32 + s]]
        if not hidden_left:
            left, right = right, left
        result[t, s] = (dot(left, right, 0, 0) * live).astype(bf16)


CHUNK = 64
CHUNKS = ROWS // CHUNK


def over_chunks(h, work):
    def step(n, carry):
        work(h, pl.ds(pl.multiple_of(n * CHUNK, CHUNK), CHUNK))
        return carry

    lax.fori_loop(0, CHUNKS, step, 0)


def layer_kernel(tok, cot, w1, w2, tab_in, output, input_grad, first_grad, second_grad,
                 tok_all, cot_all, w1_0, w1_1, w1_2, w1_3, w2_0, w2_1, w2_2, w2_3,
                 slope_all, hid, hid_other, grad, grad_other, act, model_part, second_part, first_part,
                 far_s, near_s, far_f, near_f, arrived_o, far_o, near_o, mid_o, home_o,
                 arrived_i, far_i, near_i, mid_i, home_i, tab_all, tab, send, recv, local):
    greet(Y_PEERS + X_PEERS + [CORE_PEER, ZH_PEER, ZL_PEER])
    copies = Copies(send, recv)
    core = lax.rem(lax.axis_index("col"), 2)
    first_w, second_w = (w1_0, w1_1, w1_2, w1_3), (w2_0, w2_1, w2_2, w2_3)
    on_first, on_second = pl.when(core == 0), pl.when(core == 1)
    tokens = RowGather(copies, tok, tok_all, local.at[span(14, 4)])
    cotangent = RowGather(copies, cot, cot_all, local.at[span(18, 4)])
    w1_ring = WeightGather(copies, w1, first_w)
    w2_ring = WeightGather(copies, w2, second_w)
    tokens.spread()
    tabs = [copies.start(tab_in, tab_all.at[4 - r], dy=r) for r in (1, 2, 3)]
    cotangent.spread()
    on_first(w1_ring.start)
    tab_mine = pltpu.make_async_copy(tab_in, tab_all.at[0], local.at[1])
    tab_mine.start()
    w1_mine = pltpu.make_async_copy(w1, w1_0.at[span(0, SLOTS)], local.at[2])
    w1_mine.start()
    w2_mine = pltpu.make_async_copy(w2, w2_0.at[span(0, SLOTS)], local.at[4])
    w2_mine.start()
    for weights in first_w + second_w:
        weights[SLOTS] = jnp.zeros((BLK, BLK), bf16)
    tokens.cross()
    tokens.begin()
    cotangent.cross()
    tokens.onward_up()

    @on_first
    def _():
        w1_ring.forward()
        w2_ring.start()

    tokens.second()
    tokens.onward_down()
    cotangent.begin()
    on_second(w1_ring.start)
    tokens.over_near()
    tokens.over_far()
    for copy in tabs:
        copy.wait_recv()
    tab_mine.wait()
    tab_down = pltpu.make_async_copy(tab_all, tab, local.at[5])
    tab_down.start()
    tab_down.wait()
    tokens.finish()
    w1_mine.wait()

    def rest_of_cotangent():
        cotangent.onward_down()
        cotangent.over_near()
        cotangent.over_far()

    @on_second
    def _():
        cotangent.onward_up()
        cotangent.second()
        rest_of_cotangent()
        w1_ring.forward()
        w2_ring.start()

    for r in (3, 1, 2):
        w1_ring.wait(r)

    swap = copies.reserve(HIDDEN_BLOCKS)
    back = copies.reserve(HIDDEN_BLOCKS)

    def swap_copy(h):
        return copies.at(swap + h, hid.at[h], hid_other.at[h], zl=1)

    def back_copy(h):
        return copies.at(back + h, grad.at[h], grad_other.at[h], zl=1)

    def make_hidden(h, carry):
        hid[h] = hidden_block(tok_all, first_w, tab, h, False)
        swap_copy(h).start()
        return carry

    lax.fori_loop(0, 4, make_hidden, 0)

    @on_first
    def _():
        cotangent.onward_up()
        cotangent.second()

    w2_ring.forward()
    lax.fori_loop(4, 8, make_hidden, 0)
    on_first(rest_of_cotangent)

    def make_grad(h, carry):
        grad[h] = hidden_block(cot_all, second_w, tab, h, True)
        back_copy(h).start()
        return carry

    cotangent.finish()
    w2_mine.wait()
    for r in (3, 1, 2):
        w2_ring.wait(r)
    lax.fori_loop(0, 8, make_grad, 0)

    def activate(h, rows):
        value, slope = gelu_pair(hid[h, rows].astype(f32) + hid_other[h, rows].astype(f32))
        act[h, rows] = value.astype(bf16)
        slope_all[h, rows] = slope

    for h in range(HIDDEN_BLOCKS):
        swap_copy(h).wait_recv()
        over_chunks(h, activate)

    seconds = RingReduce(copies, weight_part(second_part), far_s, near_s, "dy")

    def begin_ring(ring, hidden, rows, result, hidden_left):
        slot_grads(tab, 2, hidden, rows, result, hidden_left)
        ring.start_far()
        slot_grads(tab, 1, hidden, rows, result, hidden_left)
        ring.start_up()
        slot_grads(tab, 3, hidden, rows, result, hidden_left)
        ring.start_down()
        slot_grads(tab, 0, hidden, rows, result, hidden_left)

    begin_ring(seconds, act, cot_all, second_part, True)
    order = (2, 1, 3, 0)
    every = tuple(range(HIDDEN_BLOCKS))
    outs = {t: OutputReduce(copies, t, model_part.at[t], arrived_o.at[t], far_o.at[t], near_o.at[t], mid_o.at[t], home_o.at[t])
            for t in order}
    for t in order:
        model_tile(act, second_w, tab, t, model_part, False, every)
        outs[t].start()
    seconds.onward()
    for h in range(HIDDEN_BLOCKS):
        swap_copy(h).wait_send()

    def combine(h, rows):
        both = grad[h, rows].astype(f32) + grad_other[h, rows].astype(f32)
        hid[h, rows] = (both * slope_all[h, rows]).astype(bf16)

    def combined(*blocks):
        for h in blocks:
            back_copy(h).wait_recv()
            over_chunks(h, combine)


    def begin_outputs():
        for t in order:
            outs[t].begin()

    def onward_outputs():
        for t in order:
            outs[t].ring.onward()

    on_second(begin_outputs)
    combined(0, 1, 2, 3)

    copies.sent(*cotangent.all)
    for t in order:
        model_tile(hid, first_w, tab, t, cot_all, True, every[:4])
    on_second(onward_outputs)
    combined(4, 5)
    for t in order:
        model_tile(hid, first_w, tab, t, cot_all, True, every[4:6], True)
    combined(6, 7)
    firsts = RingReduce(copies, weight_part(first_part), far_f, near_f, "dy")
    ins = {t: OutputReduce(copies, t, cot_all.at[t], arrived_i.at[t], far_i.at[t], near_i.at[t], mid_i.at[t], home_i.at[t])
           for t in order}
    for t in order:
        model_tile(hid, first_w, tab, t, cot_all, True, every[6:], True)
        ins[t].start()
    begin_ring(firsts, hid, tok_all, first_part, False)

    @on_first
    def _():
        firsts.onward()
        begin_outputs()
        onward_outputs()

    for t in order:
        outs[t].finish()
        outs[t].across()
    for t in order:
        ins[t].begin()
    on_second(firsts.onward)
    for t in order:
        outs[t].send_home(output, local.at[6])
    for t in order:
        ins[t].ring.onward()
    seconds.finish(lambda h, n: second_part.at[0, 4 * h + n])
    second_out = pltpu.make_async_copy(second_part.at[0], second_grad, local.at[7])
    second_out.start()
    for t in order:
        ins[t].finish()
        ins[t].across()
    for t in order:
        ins[t].send_home(input_grad, local.at[8])
    firsts.finish(lambda h, n: first_part.at[0, 4 * h + n])
    first_out = pltpu.make_async_copy(first_part.at[0], first_grad, local.at[9])
    first_out.start()
    for t in order:
        outs[t].arrive()
        ins[t].arrive()
    second_out.wait()
    first_out.wait()
    for h in range(HIDDEN_BLOCKS):
        back_copy(h).wait_send()
    copies.finish()


def place_kernel(*refs):
    for source, dest in zip(refs[:4], refs[4:]):
        dest[...] = source[...]


ANY = pl.BlockSpec(memory_space=pl.ANY)
HIDDEN = (HIDDEN_BLOCKS, ROWS, BLK)
TILE = (SLOTS, BLK, BLK)
DMA = pltpu.SemaphoreType.DMA


def vmem(*dims):
    return pltpu.VMEM(dims, bf16)


def table(block_places, counts):
    places, slots = block_places[0, 0], jnp.arange(SLOTS, dtype=jnp.int32)
    live = (slots < counts[0, 0]).astype(jnp.int32)
    here = (places[None, :] == jnp.arange(32, dtype=jnp.int32)[:, None]).astype(jnp.int32) * live[None, :]
    source = SLOTS + jnp.sum(here * (slots[None, :] - SLOTS), axis=1)
    row = jnp.concatenate(
        [source, places // HIDDEN_BLOCKS, places % HIDDEN_BLOCKS, live, jnp.zeros((128 - 56,), jnp.int32)])
    return jnp.broadcast_to(row[None], (8, 128))


def per_device(tokens, w1_blocks, w2_blocks, block_places, counts, cotangent):
    weight_ring = [vmem(2, 4, BLK, BLK), vmem(2, 2, 4, BLK, BLK)]
    output_ring = [vmem(4, 4, 256, BLK), vmem(4, 2, 4, 32, BLK), vmem(4, 2, 2, 4, 32, BLK), vmem(4, 64, WIDTH), vmem(4, 32, WIDTH)]
    shapes = [jax.ShapeDtypeStruct(dims, bf16) for dims in ((128, WIDTH), (128, WIDTH), TILE, TILE)]
    results = pl.pallas_call(
        layer_kernel,
        out_shape=shapes,
        in_specs=[ANY] * 5,
        out_specs=[ANY] * 4,
        scratch_shapes=[vmem(4, 4, ROWS, BLK)] * 2
        + [vmem(SLOTS + 1, BLK, BLK)] * 8
        + [pltpu.VMEM(HIDDEN, f32)] + [vmem(*HIDDEN)] * 5
        + [vmem(4, 4, ROWS, BLK)] + [vmem(4, *TILE)] * 2
        + weight_ring * 2 + output_ring * 2
        + [pltpu.VMEM((4, 8, 128), jnp.int32), pltpu.SMEM((4, 8, 128), jnp.int32)]
        + [DMA((200,)), DMA((200,)), DMA((26,))],
        compiler_params=pltpu.CompilerParams(
            collective_id=0, has_side_effects=True, vmem_limit_bytes=62 * MIB),
    )(tokens, cotangent, w1_blocks[0, 0], w2_blocks[0, 0], table(block_places, counts))
    blocks = [pl.BlockSpec((32, WIDTH), lambda n: (n, 0))] * 2 + [pl.BlockSpec((2, BLK, BLK), lambda n: (n, 0, 0))] * 2
    output, input_grad, first_grad, second_grad = pl.pallas_call(
        place_kernel, grid=(4,), out_shape=shapes, in_specs=blocks, out_specs=blocks,
    )(*results)
    return (output, input_grad, first_grad[None, None], second_grad[None, None])


def solution(mesh):
    return jax.shard_map(
        per_device,
        mesh=mesh,
        in_specs=(
            P("col", "row"),
            P("row", "col", None, None, None),
            P("col", "row", None, None, None),
            P("row", "col", None),
            P("row", "col"),
            P("col", "row"),
        ),
        out_specs=(
            P("col", "row"),
            P("col", "row"),
            P("row", "col", None, None, None),
            P("col", "row", None, None, None),
        ),
        check_vma=False,
    )
```

```python
import functools
import math

import jax
import jax.numpy as jnp
from jax import lax
from jax.experimental import pallas as pl
from jax.experimental.pallas import tpu as pltpu
from jax.sharding import PartitionSpec as P

BLK = 256
SLOTS = 8
HIDDEN_BLOCKS = 8
QUARTER = 32
WIDTH = 1024
ROWS = 512
bf16 = jnp.bfloat16
f32 = jnp.float32

gelu_scale = math.sqrt(2.0 / math.pi)
gelu_cubic = 0.044715
MIB = 1 << 20


def gelu_pair(hidden):
    inner = gelu_scale * (hidden + gelu_cubic * hidden * hidden * hidden)
    tanh_value = jnp.tanh(inner)
    value = 0.5 * hidden * (1.0 + tanh_value)
    slope = 0.5 * (1.0 + tanh_value) + 0.5 * hidden * (
        1.0 - tanh_value * tanh_value
    ) * gelu_scale * (1.0 + 3.0 * gelu_cubic * hidden * hidden)
    return (value, slope)


def y_index():
    return lax.div(lax.axis_index("row"), 2)


def peer(dx=0, dy=0, zl=0, zh=0, core=0):
    k, j = lax.axis_index("row"), lax.axis_index("col")
    row = lax.rem(lax.div(k, 2) + dy, 4) * 2 + lax.rem(lax.rem(k, 2) + zl, 2)
    col = (
        lax.rem(lax.div(j, 4) + dx, 4) * 4
        + lax.rem(lax.rem(lax.div(j, 2), 2) + zh, 2) * 2
        + lax.rem(lax.rem(j, 2) + core, 2)
    )
    return (row, col)


Y_PEERS = [dict(dy=1), dict(dy=2), dict(dy=3)]
X_PEERS = [dict(dx=1), dict(dx=3)]
CORE_PEER, ZH_PEER, ZL_PEER = dict(core=1), dict(zh=1), dict(zl=1)


def greet(peers):
    barrier = pltpu.get_barrier_semaphore()
    for one in peers:
        pl.semaphore_signal(barrier, inc=1, device_id=peer(**one), device_id_type=pl.DeviceIdType.MESH)
    pl.semaphore_wait(barrier, len(peers))


class Copies:
    def __init__(self, send, recv):
        self.send, self.recv, self.made, self.done = send, recv, [], set()

    def make(self, src, dst, **to):
        copy = self.at(len(self.made), src, dst, **to)
        self.made.append(copy)
        return copy

    def start(self, src, dst, **to):
        copy = self.make(src, dst, **to)
        copy.start()
        return copy

    def reserve(self, count):
        first = len(self.made)
        self.made += [None] * count
        return first

    def at(self, n, src, dst, **to):
        return pltpu.make_async_remote_copy(
            src_ref=src, dst_ref=dst, send_sem=self.send.at[n], recv_sem=self.recv.at[n],
            device_id=peer(**to), device_id_type=pl.DeviceIdType.MESH,
        )

    def sent(self, *some):
        for copy in some:
            copy.wait_send()
            self.done.add(id(copy))

    def finish(self):
        for copy in self.made:
            if copy is not None and id(copy) not in self.done:
                copy.wait_send()


def span(start, size):
    return pl.ds(start, size)


LO, HI = span(0, 4), span(4, 4)


class WeightGather:
    def __init__(self, copies, own, slots):
        make = copies.make
        self.up_lo = make(own.at[LO], slots[3].at[LO], dy=1)
        self.down_hi = make(own.at[HI], slots[1].at[HI], dy=3)
        self.up_hi = make(own.at[HI], slots[3].at[HI], dy=1)
        self.down_lo = make(own.at[LO], slots[1].at[LO], dy=3)
        self.on_up = make(slots[3].at[LO], slots[2].at[LO], dy=1)
        self.on_down = make(slots[1].at[HI], slots[2].at[HI], dy=3)

    def start(self):
        for copy in (self.up_lo, self.down_hi, self.up_hi, self.down_lo):
            copy.start()

    def forward(self):
        self.up_lo.wait_recv()
        self.on_up.start()
        self.down_hi.wait_recv()
        self.on_down.start()

    def wait(self, r):
        for copy in {3: (self.up_hi,), 1: (self.down_lo,), 2: (self.on_up, self.on_down)}[r]:
            copy.wait_recv()


def part(core, x, zh, count=1):
    return (slice(None), slice(None), span(((core * 4 + x) * 2 + zh) * QUARTER, count * QUARTER))


def block(d):
    return span(d * BLK, BLK)


class RowGather:
    def __init__(self, copies, own, dest, local):
        self.mine, self.spread_copies, make = [], [], copies.make
        for r in (0, 1, 3, 2):
            rows = pl.ds(pl.multiple_of(lax.rem(y_index() + r, 4) * QUARTER, QUARTER), QUARTER)
            for d in range(4):
                piece = own.at[rows, block(d)]
                place = dest.at[(4 - r) % 4, d, span(0, QUARTER)]
                if r == 0:
                    self.mine.append(pltpu.make_async_copy(piece, place, local.at[d]))
                else:
                    self.spread_copies.append(make(piece, place, dy=r))

        def both_ways(zh):
            held = dest.at[part(0, 0, zh)]
            return make(held, dest.at[part(0, 3, zh)], dx=1), make(held, dest.at[part(0, 1, zh)], dx=3)

        self.across = make(dest.at[part(0, 0, 0)], dest.at[part(0, 0, 1)], zh=1)
        self.first, self.next = both_ways(0), both_ways(1)
        self.on_up = make(dest.at[part(0, 3, 0)], dest.at[part(0, 2, 0)], dx=1)
        self.on_down = make(dest.at[part(0, 1, 1)], dest.at[part(0, 2, 1)], dx=3)
        self.over = [make(dest.at[part(0, x, 0, 2)], dest.at[part(1, x, 0, 2)], core=1) for x in range(4)]
        self.all = self.spread_copies + [self.across, *self.first, *self.next, self.on_up, self.on_down] + self.over

    def spread(self):
        for copy in self.mine + self.spread_copies:
            copy.start()

    def cross(self):
        for copy in self.mine:
            copy.wait()
        for copy in self.spread_copies:
            copy.wait_recv()
        self.across.start()

    def begin(self):
        for copy in self.first:
            copy.start()

    def onward_up(self):
        self.first[0].wait_recv()
        self.on_up.start()

    def second(self):
        self.across.wait_recv()
        for copy in self.next:
            copy.start()
        self.over[0].start()

    def onward_down(self):
        self.next[1].wait_recv()
        self.on_down.start()

    def over_near(self):
        self.next[0].wait_recv()
        self.over[3].start()
        self.first[1].wait_recv()
        self.over[1].start()

    def over_far(self):
        self.on_up.wait_recv()
        self.on_down.wait_recv()
        self.over[2].start()

    def finish(self):
        for copy in self.over:
            copy.wait_recv()


def add_into(dst, *terms):
    def add(*refs):
        total = refs[1][...].astype(f32)
        for ref in refs[2:]:
            total = total + ref[...].astype(f32)
        refs[0][...] = total.astype(dst.dtype)

    if len(dst.shape) == 2:
        add(dst, *terms)
    else:

        def step(n, carry):
            add(*[ref.at[n] for ref in (dst,) + terms])
            return carry

        lax.fori_loop(0, dst.shape[0], step, 0)


class RingReduce:
    def __init__(self, copies, part, far, near, axis):
        self.part, self.far, self.near = part, far, near
        up, down, make = {axis: 1}, {axis: 3}, copies.make
        self.far_up = make(part(2, 0), far.at[0], **up)
        self.far_down = make(part(2, 1), far.at[1], **down)
        self.near_up = make(part(1, 1), near.at[0, 1], **up)
        self.near_down = make(part(3, 0), near.at[1, 0], **down)
        self.last_up = make(far.at[0], near.at[0, 0], **up)
        self.last_down = make(far.at[1], near.at[1, 1], **down)

    def start_far(self):
        self.far_up.start()
        self.far_down.start()

    def start_up(self):
        self.near_up.start()

    def start_down(self):
        self.near_down.start()

    def onward(self):
        self.far_up.wait_recv()
        add_into(self.far.at[0], self.far.at[0], self.part(1, 0))
        self.last_up.start()
        self.far_down.wait_recv()
        add_into(self.far.at[1], self.far.at[1], self.part(3, 1))
        self.last_down.start()

    def finish(self, dst):
        for h, arrivals in enumerate(((self.near_down, self.last_up), (self.near_up, self.last_down))):
            for copy in arrivals:
                copy.wait_recv()
            for n in range(4):
                add_into(dst(h, n), self.part(0, h).at[n], self.near.at[0, h, n], self.near.at[1, h, n])


def weight_part(partial):
    return lambda r, h: partial.at[r, (LO, HI)[h]]


class OutputReduce:
    def __init__(self, copies, t, partial, arrived, far, near, mid, home):
        self.copies, self.t, self.partial, self.arrived, self.mid, self.home = copies, t, partial, arrived, mid, home
        self.ring = RingReduce(copies, lambda r, h: arrived.at[:, span(r * 64 + h * 32, 32)], far, near, "dx")

    def start(self):
        self.over = self.copies.start(self.partial.at[:, span(256, 256)], self.arrived, core=1)

    def join(self, r):
        rows = span(64 * r, 64)
        add_into(self.arrived.at[:, rows], self.arrived.at[:, rows], self.partial.at[:, rows])

    def begin(self):
        self.over.wait_recv()
        self.join(2)
        self.ring.start_far()
        self.join(1)
        self.ring.start_up()
        self.join(3)
        self.ring.start_down()
        self.join(0)

    def finish(self):
        self.ring.finish(lambda h, n: self.mid.at[span(32 * h, 32), block(n)])

    def across(self):
        self.across_copy = self.copies.start(self.mid.at[span(32, 32)], self.home, zh=1)

    def send_home(self, output, local):
        self.across_copy.wait_recv()
        add_into(self.home, self.home, self.mid.at[span(0, 32)])
        rows = pl.ds(pl.multiple_of(y_index() * QUARTER, QUARTER), QUARTER)
        if self.t == 0:
            self.last = pltpu.make_async_copy(self.home, output.at[rows], local)
            self.last.start()
        else:
            self.last = self.copies.start(self.home, output.at[rows], dy=self.t)

    def arrive(self):
        if self.t == 0:
            self.last.wait()
        else:
            self.last.wait_recv()


def dot(a, b, da, db):
    return lax.dot_general(a, b, (((da,), (db,)), ((), ())), preferred_element_type=f32)


def hidden_block(rows, weights, tab, h, flipped):
    total = None
    for t in range(4):
        for d in range(4):
            weight = weights[t][tab[t, 0, d * HIDDEN_BLOCKS + h]]
            product = dot(rows[t, d], weight, 1, int(flipped))
            total = product if total is None else total + product
    return total.astype(bf16)


def model_tile(hidden, weights, tab, t, result, flipped, blocks, add=False):
    def step(n, carry):
        for d in (2 * n, 2 * n + 1):
            total = result[t, d].astype(f32) if add else None
            for h in blocks:
                product = dot(hidden[h], weights[t][tab[t, 0, d * HIDDEN_BLOCKS + h]], 1, int(flipped))
                total = product if total is None else total + product
            result[t, d] = total.astype(bf16)
        return carry

    lax.fori_loop(0, 2, step, 0)


def slot_grads(tab, t, hidden, rows, result, hidden_left):
    for s in range(SLOTS):
        live = tab[t, 0, 48 + s].astype(f32)
        left, right = hidden[tab[t, 0, 40 + s]], rows[t, tab[t, 0, 32 + s]]
        if not hidden_left:
            left, right = right, left
        result[t, s] = (dot(left, right, 0, 0) * live).astype(bf16)


CHUNK = 64
CHUNKS = ROWS // CHUNK


def over_chunks(h, work):
    def step(n, carry):
        work(h, pl.ds(pl.multiple_of(n * CHUNK, CHUNK), CHUNK))
        return carry

    lax.fori_loop(0, CHUNKS, step, 0)


def layer_kernel(tok, cot, w1, w2, tab_in, output, input_grad, first_grad, second_grad,
                 tok_all, cot_all, w1_0, w1_1, w1_2, w1_3, w2_0, w2_1, w2_2, w2_3,
                 slope_all, hid, hid_other, grad, grad_other, act, model_part, second_part, first_part,
                 far_s, near_s, far_f, near_f, arrived_o, far_o, near_o, mid_o, home_o,
                 arrived_i, far_i, near_i, mid_i, home_i, tab_all, tab, send, recv, local):
    greet(Y_PEERS + X_PEERS + [CORE_PEER, ZH_PEER, ZL_PEER])
    copies = Copies(send, recv)
    core = lax.rem(lax.axis_index("col"), 2)
    first_w, second_w = (w1_0, w1_1, w1_2, w1_3), (w2_0, w2_1, w2_2, w2_3)
    on_first, on_second = pl.when(core == 0), pl.when(core == 1)
    tokens = RowGather(copies, tok, tok_all, local.at[span(14, 4)])
    cotangent = RowGather(copies, cot, cot_all, local.at[span(18, 4)])
    w1_ring = WeightGather(copies, w1, first_w)
    w2_ring = WeightGather(copies, w2, second_w)
    tokens.spread()
    tabs = [copies.start(tab_in, tab_all.at[4 - r], dy=r) for r in (1, 2, 3)]
    cotangent.spread()
    on_first(w1_ring.start)
    tab_mine = pltpu.make_async_copy(tab_in, tab_all.at[0], local.at[1])
    tab_mine.start()
    w1_mine = pltpu.make_async_copy(w1, w1_0.at[span(0, SLOTS)], local.at[2])
    w1_mine.start()
    w2_mine = pltpu.make_async_copy(w2, w2_0.at[span(0, SLOTS)], local.at[4])
    w2_mine.start()
    for weights in first_w + second_w:
        weights[SLOTS] = jnp.zeros((BLK, BLK), bf16)
    tokens.cross()
    tokens.begin()
    tokens.onward_up()
    cotangent.cross()

    @on_first
    def _():
        w1_ring.forward()
        w2_ring.start()

    tokens.second()
    tokens.onward_down()
    cotangent.begin()
    on_second(w1_ring.start)
    tokens.over_near()
    tokens.over_far()
    for copy in tabs:
        copy.wait_recv()
    tab_mine.wait()
    tab_down = pltpu.make_async_copy(tab_all, tab, local.at[5])
    tab_down.start()
    tab_down.wait()
    tokens.finish()
    w1_mine.wait()

    def rest_of_cotangent():
        cotangent.onward_down()
        cotangent.over_near()
        cotangent.over_far()

    @on_second
    def _():
        cotangent.onward_up()
        cotangent.second()
        rest_of_cotangent()
        w1_ring.forward()
        w2_ring.start()

    for r in (3, 1, 2):
        w1_ring.wait(r)

    swap = copies.reserve(HIDDEN_BLOCKS)
    back = copies.reserve(HIDDEN_BLOCKS)

    def swap_copy(h):
        return copies.at(swap + h, hid.at[h], hid_other.at[h], zl=1)

    def back_copy(h):
        return copies.at(back + h, grad.at[h], grad_other.at[h], zl=1)

    def make_hidden(h, carry):
        hid[h] = hidden_block(tok_all, first_w, tab, h, False)
        swap_copy(h).start()
        return carry

    lax.fori_loop(0, 4, make_hidden, 0)

    @on_first
    def _():
        cotangent.onward_up()
        cotangent.second()

    w2_ring.forward()
    lax.fori_loop(4, 8, make_hidden, 0)
    on_first(rest_of_cotangent)

    def make_grad(h, carry):
        grad[h] = hidden_block(cot_all, second_w, tab, h, True)
        back_copy(h).start()
        return carry

    cotangent.finish()
    w2_mine.wait()
    for r in (3, 1, 2):
        w2_ring.wait(r)
    lax.fori_loop(0, 8, make_grad, 0)

    def activate(h, rows):
        value, slope = gelu_pair(hid[h, rows].astype(f32) + hid_other[h, rows].astype(f32))
        act[h, rows] = value.astype(bf16)
        slope_all[h, rows] = slope

    for h in range(HIDDEN_BLOCKS):
        swap_copy(h).wait_recv()
        over_chunks(h, activate)

    seconds = RingReduce(copies, weight_part(second_part), far_s, near_s, "dy")

    def begin_ring(ring, hidden, rows, result, hidden_left):
        slot_grads(tab, 2, hidden, rows, result, hidden_left)
        ring.start_far()
        slot_grads(tab, 1, hidden, rows, result, hidden_left)
        ring.start_up()
        slot_grads(tab, 3, hidden, rows, result, hidden_left)
        ring.start_down()
        slot_grads(tab, 0, hidden, rows, result, hidden_left)

    begin_ring(seconds, act, cot_all, second_part, True)
    order = (2, 1, 3, 0)
    every = tuple(range(HIDDEN_BLOCKS))
    outs = {t: OutputReduce(copies, t, model_part.at[t], arrived_o.at[t], far_o.at[t], near_o.at[t], mid_o.at[t], home_o.at[t])
            for t in order}
    for t in order:
        model_tile(act, second_w, tab, t, model_part, False, every)
        outs[t].start()
    seconds.onward()
    for h in range(HIDDEN_BLOCKS):
        swap_copy(h).wait_send()

    def combine(h, rows):
        both = grad[h, rows].astype(f32) + grad_other[h, rows].astype(f32)
        hid[h, rows] = (both * slope_all[h, rows]).astype(bf16)

    def combined(*blocks):
        for h in blocks:
            back_copy(h).wait_recv()
            over_chunks(h, combine)


    def begin_outputs():
        for t in order:
            outs[t].begin()

    def onward_outputs():
        for t in order:
            outs[t].ring.onward()

    on_second(begin_outputs)
    combined(0, 1, 2, 3)

    copies.sent(*cotangent.all)
    for t in order:
        model_tile(hid, first_w, tab, t, cot_all, True, every[:4])
    on_second(onward_outputs)
    combined(4, 5)
    for t in order:
        model_tile(hid, first_w, tab, t, cot_all, True, every[4:6], True)
    combined(6, 7)
    firsts = RingReduce(copies, weight_part(first_part), far_f, near_f, "dy")
    ins = {t: OutputReduce(copies, t, cot_all.at[t], arrived_i.at[t], far_i.at[t], near_i.at[t], mid_i.at[t], home_i.at[t])
           for t in order}
    for t in order:
        model_tile(hid, first_w, tab, t, cot_all, True, every[6:], True)
        ins[t].start()
    begin_ring(firsts, hid, tok_all, first_part, False)

    @on_first
    def _():
        firsts.onward()
        begin_outputs()
        onward_outputs()

    for t in order:
        outs[t].finish()
        outs[t].across()
    for t in order:
        ins[t].begin()
    on_second(firsts.onward)
    for t in order:
        outs[t].send_home(output, local.at[6])
    for t in order:
        ins[t].ring.onward()
    seconds.finish(lambda h, n: second_part.at[0, 4 * h + n])
    second_out = pltpu.make_async_copy(second_part.at[0], second_grad, local.at[7])
    second_out.start()
    for t in order:
        ins[t].finish()
        ins[t].across()
    for t in order:
        ins[t].send_home(input_grad, local.at[8])
    firsts.finish(lambda h, n: first_part.at[0, 4 * h + n])
    first_out = pltpu.make_async_copy(first_part.at[0], first_grad, local.at[9])
    first_out.start()
    for t in order:
        outs[t].arrive()
        ins[t].arrive()
    second_out.wait()
    first_out.wait()
    for h in range(HIDDEN_BLOCKS):
        back_copy(h).wait_send()
    copies.finish()


def place_kernel(*refs):
    sources, dests, held, sems = refs[:4], refs[4:8], refs[8:12], refs[12]
    loads = [pltpu.make_async_copy(a, b, sems.at[n]) for n, (a, b) in enumerate(zip(sources, held))]
    stores = [pltpu.make_async_copy(a, b, sems.at[4 + n]) for n, (a, b) in enumerate(zip(held, dests))]
    for copy in loads:
        copy.start()
    for load, store in zip(loads, stores):
        load.wait()
        store.start()
    for copy in stores:
        copy.wait()


ANY = pl.BlockSpec(memory_space=pl.ANY)
HIDDEN = (HIDDEN_BLOCKS, ROWS, BLK)
TILE = (SLOTS, BLK, BLK)
DMA = pltpu.SemaphoreType.DMA


def vmem(*dims):
    return pltpu.VMEM(dims, bf16)


def table(block_places, counts):
    places, slots = block_places[0, 0], jnp.arange(SLOTS, dtype=jnp.int32)
    live = (slots < counts[0, 0]).astype(jnp.int32)
    here = (places[None, :] == jnp.arange(32, dtype=jnp.int32)[:, None]).astype(jnp.int32) * live[None, :]
    source = SLOTS + jnp.sum(here * (slots[None, :] - SLOTS), axis=1)
    row = jnp.concatenate(
        [source, places // HIDDEN_BLOCKS, places % HIDDEN_BLOCKS, live, jnp.zeros((128 - 56,), jnp.int32)])
    return jnp.broadcast_to(row[None], (8, 128))


def per_device(tokens, w1_blocks, w2_blocks, block_places, counts, cotangent):
    weight_ring = [vmem(2, 4, BLK, BLK), vmem(2, 2, 4, BLK, BLK)]
    output_ring = [vmem(4, 4, 256, BLK), vmem(4, 2, 4, 32, BLK), vmem(4, 2, 2, 4, 32, BLK), vmem(4, 64, WIDTH), vmem(4, 32, WIDTH)]
    shapes = [jax.ShapeDtypeStruct(dims, bf16) for dims in ((128, WIDTH), (128, WIDTH), TILE, TILE)]
    results = pl.pallas_call(
        layer_kernel,
        out_shape=shapes,
        in_specs=[ANY] * 5,
        out_specs=[ANY] * 4,
        scratch_shapes=[vmem(4, 4, ROWS, BLK)] * 2
        + [vmem(SLOTS + 1, BLK, BLK)] * 8
        + [pltpu.VMEM(HIDDEN, f32)] + [vmem(*HIDDEN)] * 5
        + [vmem(4, 4, ROWS, BLK)] + [vmem(4, *TILE)] * 2
        + weight_ring * 2 + output_ring * 2
        + [pltpu.VMEM((4, 8, 128), jnp.int32), pltpu.SMEM((4, 8, 128), jnp.int32)]
        + [DMA((200,)), DMA((200,)), DMA((26,))],
        compiler_params=pltpu.CompilerParams(
            collective_id=0, has_side_effects=True, vmem_limit_bytes=62 * MIB),
    )(tokens, cotangent, w1_blocks[0, 0], w2_blocks[0, 0], table(block_places, counts))
    output, input_grad, first_grad, second_grad = pl.pallas_call(
        place_kernel, out_shape=shapes, in_specs=[ANY] * 4, out_specs=[ANY] * 4,
        scratch_shapes=[vmem(*one.shape) for one in shapes] + [DMA((8,))],
    )(*results)
    return (output, input_grad, first_grad[None, None], second_grad[None, None])


def solution(mesh):
    return jax.shard_map(
        per_device,
        mesh=mesh,
        in_specs=(
            P("col", "row"),
            P("row", "col", None, None, None),
            P("col", "row", None, None, None),
            P("row", "col", None),
            P("row", "col"),
            P("col", "row"),
        ),
        out_specs=(
            P("col", "row"),
            P("col", "row"),
            P("row", "col", None, None, None),
            P("col", "row", None, None, None),
        ),
        check_vma=False,
    )
```
